32 devices in a mesh: segment: 2 (over x), seq: 8 (over z, core), tensor: 2 (over y).
Axes of the slice: x: 2, y: 2, z: 4, core: 2. Of those that a mesh axis runs over, the one named last changes fastest.
Arguments:
- vision_states: bfloat16 [1536, 7680], P(('segment', 'seq'), 'tensor'), may hold values from -6 to 6
- kv_weight: bfloat16 [7680, 2048], P('tensor'), may hold values from -0.09375 to 0.09375
- key_gain: float32 [128], replicated, may hold values from 0.5 to 1.5
- queries: bfloat16 [4096, 8, 1024], P('seq', 'tensor', 'segment'), may hold values from -700 to 700
- tile_tokens: int32 [4], replicated, may hold values from 192 to 384, as said below
- text_tiles: int32 [4096, 2], P('seq'), may hold values from 0 to 4, as said below
Outputs:
- attended: bfloat16 [4096, 8, 1024], P('seq', 'tensor', 'segment')
The draws below stay inside these ranges and needn't reach their ends.
Inputs may be any that keep to these rules, and one draw needn't show every extreme that they name: The valid tokens of tile i are its first tile_tokens[i] positions of 384; some tile is full. Text token r sees tiles text_tiles[r, 0] to text_tiles[r, 1] - 1, with text_tiles[r, 0] <= text_tiles[r, 1]; an empty range means it sees no image.
All inputs are finite; a program needn't handle non-finite values.
Results may differ from the reference program's by a relative error of at most 0.012.
The reference program's roundings to bfloat16 on the way (of `keys`, `values` and `weights`) count: a program that leaves them out, or rounds other values in their place, can miss the bound.
Values may be sent and summed in bfloat16 or wider, within the bound.
No kernel may reach another device: no remote copies, remote signals or barrier semaphores. Data moves between devices by JAX's collectives and lax.ppermute only.
A program may use at most 128 MiB of HBM per device.

```python
import math
import jax
import jax.numpy as jnp
from jax import lax

DV = 7680
KVH = 8
HD = 128
TILES = 4
VT = 1536
TT = 4096
TILE_LEN = 384
GROUP = 8


def draw_queries(key, part):
    first_key = jax.random.fold_in(key, 0)
    shape = (TT, KVH, GROUP * HD)
    base = jax.random.normal(first_key, shape, jnp.float32) * 2.5
    return jnp.clip(base, -15.0, 15.0).astype(jnp.bfloat16)


def draw_tile_tokens(key, part):
    first_key, second_key = jax.random.split(key)
    counts = jax.random.randint(first_key, (TILES,), TILE_LEN // 2, TILE_LEN + 1, dtype=jnp.int32)
    full_tile = jax.random.randint(second_key, (), 0, TILES, dtype=jnp.int32)
    return jnp.where(jnp.arange(TILES, dtype=jnp.int32) == full_tile, TILE_LEN, counts).astype(jnp.int32)


def draw_text_tiles(key, part):
    first_key, second_key, third_key = jax.random.split(key, 3)
    lower = jax.random.randint(first_key, (TT,), 0, TILES, dtype=jnp.int32)
    upper = jax.random.randint(second_key, (TT,), lower + 1, TILES + 1, dtype=jnp.int32)
    unseen = jax.random.randint(third_key, (TT,), 0, 8, dtype=jnp.int32) == 0
    upper = jnp.where(unseen, lower, upper)
    return jnp.stack([lower, upper], axis=1).astype(jnp.int32)


def spiked(values, stream_key, source, target, blocks, factor):
    def block_of(axis_at):
        return (jnp.arange(values.shape[axis_at]) // (values.shape[axis_at] // blocks)).reshape((-1,) + (1,) * (values.ndim - 1 - axis_at))

    one_side = jax.random.permutation(stream_key, blocks)[block_of(target)]
    far = (block_of(target) + blocks // 2) % blocks
    return jnp.where((block_of(source) == one_side) | (block_of(source) == far), factor * values, values)


def steps_of(key, extent, cuts, low, high):
    loudness = 1.0
    for position, blocks in cuts:
        steps = jax.random.uniform(jax.random.fold_in(jax.random.fold_in(key, 6), position), (blocks,), jnp.float32, low / len(cuts), high / len(cuts))
        loudness = loudness * jnp.repeat(jnp.exp(steps), extent[position] // blocks).reshape((-1,) + (1,) * (len(extent) - 1 - position))
    return loudness


def scatter_about(rng, shape, spread, reach, pieces=(), kind=jnp.bfloat16):
    entries = jax.random.normal(rng, shape, jnp.float32) * spread
    if len(pieces) > 0:
        entries = steps_of(rng, shape, pieces, -0.22, 0.18) * entries
    return jnp.clip(entries, min=-reach, max=reach).astype(kind)


def gaussian_with(own_key, dims, scale, bound, cuts, heavy, kind=jnp.bfloat16):
    drawn = scale * jax.random.normal(own_key, dims, jnp.float32)
    if cuts:
        drawn = drawn * steps_of(own_key, dims, cuts, -0.22, 0.18)
    return jnp.clip(spiked(drawn, jax.random.fold_in(own_key, 3), *heavy), -bound, bound).astype(kind)


def setup_inputs(seed: int = 0) -> dict:
    seeds = jax.random.split(jax.random.key(seed), 7)
    vision_states = scatter_about(seeds[0], (VT, DV), 1.0, 6.0, ((0, 16), (1, 2)))
    kv_weight = gaussian_with(seeds[1], (DV, KVH * 2 * HD), DV ** -0.5, 0.09375, ((0, 2),), (0, 1, 2, 2.0))
    key_gain = jnp.clip(jax.random.uniform(seeds[2], (HD,), jnp.float32, 0.5, 1.5), 0.5, 1.5)
    queries = draw_queries(jax.random.fold_in(seeds[6], 71), 0)
    tile_tokens = draw_tile_tokens(jax.random.fold_in(seeds[6], 71), 0)
    text_tiles = draw_text_tiles(jax.random.fold_in(seeds[6], 71), 0)
    return dict(vision_states=vision_states, kv_weight=kv_weight, key_gain=key_gain, queries=queries, tile_tokens=tile_tokens, text_tiles=text_tiles)


def reference(vision_states, kv_weight, key_gain, queries, tile_tokens, text_tiles):
    projected = jnp.dot(vision_states, kv_weight, preferred_element_type=jnp.float32)
    projected = projected.reshape(VT, KVH, 2 * HD)
    keys_raw = projected[:, :, :HD]
    mean_sq = lax.optimization_barrier(jnp.mean(keys_raw * keys_raw, axis=-1, keepdims=True))
    keys = (keys_raw * lax.rsqrt(mean_sq + 1e-05) * key_gain).astype(jnp.bfloat16)
    values = projected[:, :, HD:].astype(jnp.bfloat16)
    positions = jnp.arange(VT, dtype=jnp.int32)
    tile_ids = positions // TILE_LEN
    key_valid = positions % TILE_LEN < tile_tokens[tile_ids]
    score_scale = HD ** (-0.5)
    block_rows = math.gcd(TT, 512)
    query_blocks = queries.reshape(TT // block_rows, block_rows, KVH, GROUP, HD)
    lower_blocks = text_tiles[:, 0].reshape(TT // block_rows, block_rows)
    upper_blocks = text_tiles[:, 1].reshape(TT // block_rows, block_rows)
    keys_heads = jnp.transpose(keys, (1, 0, 2))
    values_heads = jnp.transpose(values, (1, 0, 2))

    def one_block(packed):
        query_block, lower, upper = packed
        visible = key_valid[None, :] & (tile_ids[None, :] >= lower[:, None]) & (tile_ids[None, :] < upper[:, None])
        unseen = (upper <= lower).astype(jnp.float32)

        def one_head(head_pack):
            query_head, key_head, value_head = head_pack
            scores = jnp.einsum('rgd,nd->rgn', query_head.astype(jnp.float32), key_head.astype(jnp.float32)) * score_scale
            key_mask = visible[:, None, :]
            masked = jnp.where(key_mask, scores, -1e+30)
            row_max = lax.optimization_barrier(jnp.max(masked, axis=-1, keepdims=True))
            expterm = jnp.where(key_mask, jnp.exp(masked - row_max), 0.0)
            denominator = lax.optimization_barrier(jnp.sum(expterm, axis=-1))
            weights = expterm.astype(jnp.bfloat16)
            numerator = jnp.einsum('rgn,nd->rgd', weights.astype(jnp.float32), value_head.astype(jnp.float32))
            return numerator / (denominator + unseen[:, None])[:, :, None]
        query_heads = jnp.transpose(query_block, (1, 0, 2, 3))
        outputs = lax.map(one_head, (query_heads, keys_heads, values_heads))
        return jnp.transpose(outputs, (1, 0, 2, 3)).reshape(block_rows, KVH, GROUP * HD)
    result = lax.map(one_block, (query_blocks, lower_blocks, upper_blocks))
    return result.reshape(TT, KVH, GROUP * HD).astype(jnp.bfloat16)
```

```python
import functools

import jax
import jax.numpy as jnp
from jax import lax
from jax.experimental import pallas as pl
from jax.experimental.pallas import tpu as pltpu
from jax.sharding import PartitionSpec as P

MASKED = -1e30
LOG2E = 1.4426950408889634
VMEM = pl.BlockSpec(memory_space=pltpu.VMEM)
SMEM = pl.BlockSpec(memory_space=pltpu.SMEM)
ANY = pl.BlockSpec(memory_space=pl.ANY)


def project_kernel(block_ref, vision_ref, weight_ref, out_ref):
    out_ref[...] = jnp.dot(vision_ref[...], weight_ref[...], preferred_element_type=jnp.float32)


def project(vision, weight, first_block, block_cols, blocks):
    rows, depth = vision.shape
    return pl.pallas_call(
        project_kernel,
        grid_spec=pltpu.PrefetchScalarGridSpec(
            num_scalar_prefetch=1,
            grid=(blocks,),
            in_specs=[
                pl.BlockSpec((rows, depth), lambda i, first: (0, 0)),
                pl.BlockSpec((depth, block_cols), lambda i, first: (0, first[0] + i)),
            ],
            out_specs=pl.BlockSpec((rows, block_cols), lambda i, first: (0, i)),
        ),
        out_shape=jax.ShapeDtypeStruct((rows, blocks * block_cols), jnp.float32),
        compiler_params=pltpu.CompilerParams(vmem_limit_bytes=32 * 1024 * 1024),
        cost_estimate=pl.CostEstimate(
            flops=2 * rows * depth * blocks * block_cols,
            bytes_accessed=2 * depth * blocks * block_cols,
            transcendentals=0,
        ),
    )(first_block.reshape(1), vision, weight)


def finish_kernel(heads, dim, own_ref, other_ref, gain_ref, out_ref):
    for head in range(heads):
        at = head * 2 * dim
        keys = own_ref[:, at : at + dim] + other_ref[:, at : at + dim]
        mean_sq = jnp.mean(keys * keys, axis=-1, keepdims=True)
        keys = keys * lax.rsqrt(mean_sq + 1e-05) * gain_ref[...]
        values = own_ref[:, at + dim : at + 2 * dim] + other_ref[:, at + dim : at + 2 * dim]
        out_ref[head, :, :dim] = keys.astype(jnp.bfloat16)
        out_ref[head, :, dim:] = values.astype(jnp.bfloat16)


def finish(own, other, gain, heads, dim):
    rows = own.shape[0]
    return pl.pallas_call(
        functools.partial(finish_kernel, heads, dim),
        in_specs=[VMEM, VMEM, VMEM],
        out_specs=VMEM,
        out_shape=jax.ShapeDtypeStruct((heads, rows, 2 * dim), jnp.bfloat16),
        cost_estimate=pl.CostEstimate(flops=8 * own.size, bytes_accessed=10 * own.size, transcendentals=rows),
    )(own, other, gain.reshape(1, dim))


def attend_kernel(heads, group, dim, tiles, block_rows, pieces, place_ref, tokens_ref, *refs):
    kv_refs = refs[:pieces]
    q_ref, range_ref, out_ref, k_ref, v_ref, qm_ref, s_ref, sems = refs[pieces:]
    text_rows = q_ref.shape[1]
    total = k_ref.shape[1]
    piece_rows = kv_refs[0].shape[1]
    tile_len = total // tiles
    copies = []
    for piece in range(pieces):
        at = pl.multiple_of(place_ref[piece] * piece_rows, piece_rows)
        for part, into in enumerate((k_ref.at[:, pl.ds(at, piece_rows), pl.ds(0, dim)], v_ref.at[:, pl.ds(at, piece_rows), :])):
            copy = pltpu.make_async_copy(kv_refs[piece].at[:, :, pl.ds(part * dim, dim)], into, sems.at[piece, part])
            copy.start()
            copies.append(copy)
    lanes = lax.broadcasted_iota(jnp.int32, (text_rows, dim), 1)
    lower, upper = range_ref[:, 0:1], range_ref[:, 1:2]
    hidden = (lanes < lower) | (lanes >= upper) | (lanes >= tiles)
    qm_ref[...] = jnp.where(hidden & (lanes <= tiles), 1.0, 0.0).astype(jnp.bfloat16)
    key_lanes = lax.broadcasted_iota(jnp.int32, (tile_len, dim), 1)
    key_place = lax.broadcasted_iota(jnp.int32, (tile_len, dim), 0)
    for tile in range(tiles):
        off = (key_lanes == tile) | ((key_lanes == tiles) & (key_place >= tokens_ref[tile]))
        for head in range(heads):
            k_ref[head, tile * tile_len : (tile + 1) * tile_len, dim:] = jnp.where(off, MASKED, 0.0).astype(jnp.bfloat16)
    for copy in copies:
        copy.wait()
    row_blocks = text_rows // block_rows
    steps = heads * group * row_blocks
    scale = LOG2E * dim ** (-0.5)

    def where(step):
        head = step // (group * row_blocks)
        rest = step % (group * row_blocks)
        return head, rest // row_blocks, rest % row_blocks

    def score(step, slot):
        head, member, block = where(step)
        rows = pl.ds(block * block_rows, block_rows)
        cols = pl.ds(pl.multiple_of(member * dim, dim), dim)
        q = jnp.concatenate([q_ref[head, rows, cols], qm_ref[rows, :]], axis=1)
        s_ref[slot] = lax.dot_general(
            q, k_ref[head], (((1,), (1,)), ((), ())), preferred_element_type=jnp.float32
        )

    def weigh(step, slot):
        head, member, block = where(step)
        rows = pl.ds(block * block_rows, block_rows)
        cols = pl.ds(pl.multiple_of(member * dim, dim), dim)
        scores = s_ref[slot]
        row_max = jnp.max(scores, axis=1, keepdims=True)
        terms = jnp.exp2((scores - row_max) * scale)
        denominator = jnp.sum(terms, axis=1, keepdims=True)
        summed = jnp.dot(terms.astype(jnp.bfloat16), v_ref[head], preferred_element_type=jnp.float32)
        seen = range_ref[rows, 1:2] > range_ref[rows, 0:1]
        attended = jnp.where(seen, summed / denominator, 0.0)
        out_ref[head, rows, cols] = attended.astype(jnp.bfloat16)

    score(0, 0)

    @pl.loop(0, steps // 2)
    def _(pair):
        step = pair * 2
        score(step + 1, 1)
        weigh(step, 0)
        score(jnp.minimum(step + 2, steps - 1), 0)
        weigh(step + 1, 1)


def attend(q, kv, places, tokens, text_tiles, tiles):
    heads, text_rows, width = q.shape
    dim = kv[0].shape[2] // 2
    group = width // dim
    total = sum(piece.shape[1] for piece in kv)
    block_rows = min(256, text_rows)
    cells = heads * group * text_rows * total
    return pl.pallas_call(
        functools.partial(attend_kernel, heads, group, dim, tiles, block_rows, len(kv)),
        in_specs=[SMEM, SMEM] + [ANY] * len(kv) + [VMEM, VMEM],
        out_specs=VMEM,
        out_shape=jax.ShapeDtypeStruct(q.shape, jnp.bfloat16),
        scratch_shapes=[
            pltpu.VMEM((heads, total, 2 * dim), jnp.bfloat16),
            pltpu.VMEM((heads, total, dim), jnp.bfloat16),
            pltpu.VMEM((text_rows, dim), jnp.bfloat16),
            pltpu.VMEM((2, block_rows, total), jnp.float32),
            pltpu.SemaphoreType.DMA((len(kv), 2)),
        ],
        compiler_params=pltpu.CompilerParams(vmem_limit_bytes=48 * 1024 * 1024),
        cost_estimate=pl.CostEstimate(
            flops=4 * cells * dim, bytes_accessed=4 * q.size + 4 * heads * total * dim, transcendentals=cells
        ),
    )(places, tokens, *kv, q, text_tiles)


def shards(vision_states, kv_weight, key_gain, queries, tile_tokens, text_tiles):
    dim = key_gain.shape[0]
    vision_rows = vision_states.shape[0]
    all_heads = kv_weight.shape[1] // (2 * dim)
    tensor, segment, seq = lax.axis_size("tensor"), lax.axis_size("segment"), lax.axis_size("seq")
    heads = all_heads // tensor
    tiles = tile_tokens.shape[0]
    q = jnp.transpose(queries, (1, 0, 2))
    if tensor == 2 and segment == 2 and seq == 8:
        kv, places = exchange(vision_states, kv_weight, key_gain, heads, dim)
    else:
        weight_heads = kv_weight.reshape(kv_weight.shape[0], all_heads, 2 * dim)
        partial = jnp.einsum("rd,dch->crh", vision_states, weight_heads, preferred_element_type=jnp.float32)
        sums = lax.psum_scatter(partial, "tensor", scatter_dimension=0, tiled=True)
        keys = sums[:, :, :dim]
        mean_sq = jnp.mean(keys * keys, axis=-1, keepdims=True)
        keys = keys * lax.rsqrt(mean_sq + 1e-05) * key_gain
        block = jnp.concatenate([keys, sums[:, :, dim:]], axis=-1).astype(jnp.bfloat16)
        kv = [lax.all_gather(block, ("segment", "seq"), axis=1, tiled=True)]
        places = jnp.zeros((1,), jnp.int32)
    attended = attend(q, kv, places, tile_tokens, text_tiles, tiles)
    return jnp.transpose(attended, (1, 0, 2))


def exchange(vision_states, kv_weight, key_gain, heads, dim):
    me_tensor, me_segment, me_seq = lax.axis_index("tensor"), lax.axis_index("segment"), lax.axis_index("seq")
    cols = heads * 2 * dim
    block_cols = 2 * dim
    theirs = project(vision_states, kv_weight, (1 - me_tensor) * heads, block_cols, heads)
    arrived = lax.ppermute(theirs, "tensor", [(0, 1), (1, 0)])
    mine = project(vision_states, kv_weight, me_tensor * heads, block_cols, heads)
    block = finish(mine, arrived, key_gain, heads, dim)
    lane = [block] + [lax.ppermute(block, "seq", [(s, s ^ (2 * far)) for s in range(8)]) for far in (1, 2, 3)]
    lane += [lax.ppermute(piece, "segment", [(0, 1), (1, 0)]) for piece in lane]
    both = lane + [lax.ppermute(piece, "seq", [(s, s ^ 1) for s in range(8)]) for piece in lane]
    places = jnp.stack(
        [
            (me_segment ^ side) * 8 + (me_seq ^ (2 * far + core))
            for core in range(2)
            for side in range(2)
            for far in range(4)
        ]
    ).astype(jnp.int32)
    return both, places


def solution(mesh):
    placed = (
        P(("segment", "seq"), "tensor"),
        P("tensor", None),
        P(),
        P("seq", "tensor", "segment"),
        P(),
        P("seq", None),
    )
    return jax.shard_map(
        shards, mesh=mesh, in_specs=placed, out_specs=P("seq", "tensor", "segment"), check_vma=False
    )
```

```python
import functools

import jax
import jax.numpy as jnp
from jax import lax
from jax.experimental import pallas as pl
from jax.experimental.pallas import tpu as pltpu
from jax.sharding import PartitionSpec as P

MASKED = -1e30
CHUNKS = 1
STORES = 4
LOG2E = 1.4426950408889634
BLOCK_ROWS = 128
LARGE_VMEM = 52 * 1024 * 1024
MIDDLE_VMEM = 44 * 1024 * 1024
SMALL_VMEM = 16 * 1024 * 1024
VMEM = pl.BlockSpec(memory_space=pltpu.VMEM)
SMEM = pl.BlockSpec(memory_space=pltpu.SMEM)
ANY = pl.BlockSpec(memory_space=pl.ANY)
HBM = pl.BlockSpec(memory_space=pltpu.HBM)
ROWS_BY_ROWS = (((1,), (1,)), ((), ()))
COLS_BY_COLS = (((0,), (0,)), ((), ()))


def lasting(microseconds):
    return pl.CostEstimate(flops=0, bytes_accessed=int(3.6e6 * microseconds), transcendentals=0)


def project_kernel(pieces, block_ref, vision_hbm_ref, weight_ref, *refs):
    count = block_ref.shape[0]
    out_hbm_refs, (vision_ref, held_ref, out_ref, vision_sem, sems, out_sems) = refs[:count], refs[count:]
    depth, cols = held_ref.shape[1:]
    load = pltpu.make_async_copy(vision_hbm_ref, vision_ref, vision_sem)
    load.start()
    copies = []
    for step in range(count * pieces):
        which, piece = divmod(step, pieces)
        across = pl.ds(pl.multiple_of(block_ref[which] * cols, cols), cols)
        copies.append(
            pltpu.make_async_copy(weight_ref.at[pl.ds(piece * depth, depth), across], held_ref.at[step], sems.at[step])
        )
        copies[-1].start()
    load.wait()
    stores = []
    for which in range(count):
        total = None
        for piece in range(pieces):
            copies[which * pieces + piece].wait()
            part = vision_ref[:, piece * depth : (piece + 1) * depth]
            product = jnp.dot(part, held_ref[which * pieces + piece], preferred_element_type=jnp.float32)
            total = product if piece == 0 else total + product
        out_ref[which] = total
        stores.append(pltpu.make_async_copy(out_ref.at[which], out_hbm_refs[which], out_sems.at[which]))
        stores[-1].start()
    for store in stores:
        store.wait()


def project(vision, weight, blocks, cols):
    rows, depth = vision.shape
    count = len(blocks)
    pieces = next(parts for parts in (5, 3, 2, 1) if depth % (parts * 128) == 0)
    return pl.pallas_call(
        functools.partial(project_kernel, pieces),
        in_specs=[SMEM, ANY, ANY],
        out_specs=[ANY] * count,
        out_shape=[jax.ShapeDtypeStruct((rows, cols), jnp.float32)] * count,
        scratch_shapes=[
            pltpu.VMEM((rows, depth), jnp.bfloat16),
            pltpu.VMEM((count * pieces, depth // pieces, cols), jnp.bfloat16),
            pltpu.VMEM((count, rows, cols), jnp.float32),
            pltpu.SemaphoreType.DMA,
            pltpu.SemaphoreType.DMA((count * pieces,)),
            pltpu.SemaphoreType.DMA((count,)),
        ],
        compiler_params=pltpu.CompilerParams(vmem_limit_bytes=LARGE_VMEM),
        cost_estimate=lasting(2 + 1.2 * count),
    )(jnp.stack(blocks), vision, weight)


def finish_kernel(heads, dim, own_ref, other_ref, gain_ref, out_ref):
    for head in range(heads):
        at = head * 2 * dim
        keys = own_ref[:, at : at + dim] + other_ref[:, at : at + dim]
        mean_sq = jnp.mean(keys * keys, axis=-1, keepdims=True)
        keys = keys * lax.rsqrt(mean_sq + 1e-05) * gain_ref[...]
        values = own_ref[:, at + dim : at + 2 * dim] + other_ref[:, at + dim : at + 2 * dim]
        out_ref[head, :, :dim] = keys.astype(jnp.bfloat16)
        out_ref[head, :, dim:] = values.astype(jnp.bfloat16)


def finish(own, other, gain, heads, dim):
    rows = own.shape[0]
    return pl.pallas_call(
        functools.partial(finish_kernel, heads, dim),
        in_specs=[VMEM, VMEM, VMEM],
        out_specs=VMEM,
        out_shape=jax.ShapeDtypeStruct((heads, rows, 2 * dim), jnp.bfloat16),
        compiler_params=pltpu.CompilerParams(vmem_limit_bytes=SMALL_VMEM),
        cost_estimate=lasting(1.5),
    )(own, other, gain.reshape(1, dim))


def sort_kernel(tiles, group, q_ref, range_rows_ref, sorted_ref, hidden_ref, back_ref, hull_ref):
    rows, heads, width = q_ref.shape
    dim = width // group

    def order(lower, upper, at):
        key = jnp.where(upper > lower, (tiles - 1 - lower) * (tiles + 1) + tiles - upper, -1)
        return key * rows + at

    lower_row, upper_row = range_rows_ref[0:1, :], range_rows_ref[1:2, :]
    columns = jnp.concatenate([lower_row, upper_row] * 4, axis=0).astype(jnp.float32).T.astype(jnp.int32)
    lower, upper = columns[:, 0:1], columns[:, 1:2]
    order_col = order(lower, upper, lax.broadcasted_iota(jnp.int32, (rows, 1), 0))
    order_row = order(lower_row, upper_row, lax.broadcasted_iota(jnp.int32, (1, rows), 1))
    rank_row = jnp.sum(jnp.where(order_col < order_row, 1.0, 0.0), axis=0, keepdims=True).astype(jnp.int32)
    rank_col = jnp.sum(jnp.where(order_row < order_col, 1.0, 0.0), axis=1, keepdims=True).astype(jnp.int32)
    into = jnp.where(lax.broadcasted_iota(jnp.int32, (rows, rows), 0) == rank_row, 1.0, 0.0).astype(jnp.bfloat16)
    back = jnp.where(lax.broadcasted_iota(jnp.int32, (rows, rows), 1) == rank_col, 1.0, 0.0).astype(jnp.bfloat16)
    back_ref[...] = back
    seen_row = upper_row > lower_row
    blocks = rows // BLOCK_ROWS
    for block in range(blocks):
        inside = seen_row & (rank_row >= block * BLOCK_ROWS) & (rank_row < (block + 1) * BLOCK_ROWS)
        hull_ref[0, block] = jnp.min(jnp.where(inside, lower_row, tiles).astype(jnp.float32)).astype(jnp.int32)
        hull_ref[1, block] = jnp.max(jnp.where(inside, upper_row, 0).astype(jnp.float32)).astype(jnp.int32)
    hull_ref[2, 0] = jnp.sum(jnp.where(seen_row, 0.0, 1.0)).astype(jnp.int32)
    lanes = lax.broadcasted_iota(jnp.int32, (rows, dim), 1)
    unseen = (lanes < tiles) & ((lanes < lower) | (lanes >= upper)) | (lanes == tiles)
    hidden = jnp.where(unseen, 1.0, 0.0).astype(jnp.bfloat16)
    hidden_ref[...] = jnp.dot(into, hidden, preferred_element_type=jnp.float32).astype(jnp.bfloat16)
    q_heads = jnp.transpose(q_ref[...], (1, 0, 2))
    for head in range(heads):
        moved = jnp.dot(into, q_heads[head], preferred_element_type=jnp.float32).astype(jnp.bfloat16)
        for block in range(blocks):
            for member in range(group):
                at = (block * group + member) * BLOCK_ROWS
                sorted_ref[head, at : at + BLOCK_ROWS, :] = moved[
                    block * BLOCK_ROWS : (block + 1) * BLOCK_ROWS, member * dim : (member + 1) * dim
                ]


def sort_rows(queries, text_tiles, tiles, dim):
    rows, heads, width = queries.shape
    group = width // dim
    return pl.pallas_call(
        functools.partial(sort_kernel, tiles, group),
        in_specs=[VMEM, VMEM],
        out_specs=[VMEM, VMEM, VMEM, SMEM],
        out_shape=[
            jax.ShapeDtypeStruct((heads, rows * group, dim), jnp.bfloat16),
            jax.ShapeDtypeStruct((rows, dim), jnp.bfloat16),
            jax.ShapeDtypeStruct((rows, rows), jnp.bfloat16),
            jax.ShapeDtypeStruct((3, rows // BLOCK_ROWS), jnp.int32),
        ],
        compiler_params=pltpu.CompilerParams(vmem_limit_bytes=MIDDLE_VMEM),
        cost_estimate=lasting(5),
    )(queries, text_tiles.T)


def attend_kernel(shape, offsets, earlier, last, home_ref, tokens_ref, hull_ref, *refs):
    heads, first_head, blocks, group, dim, tiles, tile_len = shape
    pieces = len(offsets)
    kv_refs, refs = refs[:pieces], refs[pieces:]
    done_refs, refs = refs[:earlier], refs[earlier:]
    q_hbm_ref, hidden_hbm_ref, back_hbm_ref, result_hbm_ref = refs[:4]
    q_ref, hidden_ref, back_ref, done_ref, result_ref, k_ref, v_ref, turned_ref, sems, load_sems, store_sems = refs[4:]
    piece_rows = kv_refs[0].shape[1]
    columns = group * BLOCK_ROWS
    scale = LOG2E * dim ** (-0.5)
    copies = []
    for piece in range(pieces):
        at = pl.multiple_of((home_ref[0] ^ offsets[piece]) * piece_rows, piece_rows)
        into = k_ref.at[:, pl.ds(at, piece_rows), pl.ds(0, dim)], v_ref.at[:, pl.ds(at, piece_rows), :]
        for part in range(2):
            source = kv_refs[piece].at[:, :, pl.ds(part * dim, dim)]
            copies.append(pltpu.make_async_copy(source, into[part], sems.at[piece, part]))
            copies[-1].start()
    loads = [(q_hbm_ref.at[pl.ds(first_head, heads)], q_ref), (hidden_hbm_ref, hidden_ref), (back_hbm_ref, back_ref)]
    loads += [(ref, done_ref.at[pl.ds(i * heads, heads)]) for i, ref in enumerate(done_refs)]
    loads = [pltpu.make_async_copy(*ends, load_sems.at[i]) for i, ends in enumerate(loads)]
    for load in loads:
        load.start()
    lanes = lax.broadcasted_iota(jnp.int32, (tile_len, dim), 1)
    place = lax.broadcasted_iota(jnp.int32, (tile_len, dim), 0)
    for tile in range(tiles):
        off = (lanes == tile) | ((lanes == tiles) & (place >= tokens_ref[tile]))
        off = jnp.where(off, MASKED, 0.0).astype(jnp.bfloat16)
        for head in range(heads):
            k_ref[head, tile * tile_len : (tile + 1) * tile_len, dim:] = off
    for copy in [*copies, *loads[:2]]:
        copy.wait()

    def work(block, first, count):
        here = pl.ds(pl.multiple_of(block * BLOCK_ROWS, BLOCK_ROWS), BLOCK_ROWS)
        if count == 0:
            turned_ref[:, :, here] = jnp.zeros((heads, group * dim, BLOCK_ROWS), jnp.bfloat16)
            return
        rows = pl.ds(pl.multiple_of(block * columns, columns), columns)
        span = pl.ds(pl.multiple_of(first * tile_len, tile_len), count * tile_len)
        hidden = jnp.concatenate([hidden_ref[here, :]] * group, axis=0)
        row = lax.broadcasted_iota(jnp.int32, (1, columns), 1) % BLOCK_ROWS + block * BLOCK_ROWS
        scores = [
            lax.dot_general(
                k_ref[head, span, :],
                jnp.concatenate([q_ref[head, rows, :], hidden], axis=1),
                ROWS_BY_ROWS,
                preferred_element_type=jnp.float32,
            )
            for head in range(heads)
        ]
        for head in range(heads):
            row_max = jnp.max(scores[head], axis=0, keepdims=True)
            terms = jnp.exp2((scores[head] - row_max) * scale)
            denominator = jnp.sum(terms, axis=0, keepdims=True)
            summed = lax.dot_general(
                v_ref[head, span, :], terms.astype(jnp.bfloat16), COLS_BY_COLS, preferred_element_type=jnp.float32
            )
            inverse = jnp.where(row >= hull_ref[2, 0], 1.0 / denominator, 0.0)
            attended = (summed * inverse).astype(jnp.bfloat16)
            for member in range(group):
                turned_ref[head, member * dim : (member + 1) * dim, here] = attended[
                    :, member * BLOCK_ROWS : (member + 1) * BLOCK_ROWS
                ]

    @pl.loop(0, blocks)
    def _(block):
        first = hull_ref[0, block]
        seen = jnp.maximum(hull_ref[1, block] - first, 0)
        for count in range(tiles + 1):

            @pl.when(seen == count)
            def _():
                work(block, first, count)

    for load in loads[2:]:
        load.wait()
    if not last:
        store = pltpu.make_async_copy(turned_ref, result_hbm_ref, store_sems.at[0])
        store.start()
        store.wait()
        return
    stores = []
    rows = back_ref.shape[0] // STORES
    for part in range(STORES):
        here = pl.ds(part * rows, rows)
        back = back_ref[here, :]
        whole = [
            lax.dot_general(back, turned, ROWS_BY_ROWS, preferred_element_type=jnp.float32).astype(jnp.bfloat16)
            for turned in [done_ref[i] for i in range(first_head)] + [turned_ref[head] for head in range(heads)]
        ]
        result_ref[here] = jnp.transpose(jnp.stack(whole, axis=0), (1, 0, 2))
        stores.append(pltpu.make_async_copy(result_ref.at[here], result_hbm_ref.at[here], store_sems.at[part]))
        stores[-1].start()
    for store in stores:
        store.wait()


def attend(text, first, kv, offsets, home, tokens, tile_len, done, last):
    q, hidden, back, hull = text
    heads, dim = kv[0].shape[0], kv[0].shape[2] // 2
    text_rows, blocks = back.shape[0], hull.shape[1]
    group, tiles = q.shape[1] // text_rows, tokens.shape[0]
    width = group * dim
    total = sum(piece.shape[1] for piece in kv)
    whole = (text_rows, q.shape[0], width) if last else (heads, width, text_rows)
    return pl.pallas_call(
        functools.partial(attend_kernel, (heads, first, blocks, group, dim, tiles, tile_len), offsets, len(done), last),
        in_specs=[SMEM] * 3 + [ANY] * len(kv) + [HBM] * (len(done) + 3),
        out_specs=ANY,
        out_shape=jax.ShapeDtypeStruct(whole, jnp.bfloat16),
        scratch_shapes=[
            pltpu.VMEM((heads, *q.shape[1:]), jnp.bfloat16),
            pltpu.VMEM(hidden.shape, jnp.bfloat16),
            pltpu.VMEM(back.shape, jnp.bfloat16),
            pltpu.VMEM((max(first, 1), width, text_rows), jnp.bfloat16),
            pltpu.VMEM((text_rows, q.shape[0], width) if last else (8, 128), jnp.bfloat16),
            pltpu.VMEM((heads, total, 2 * dim), jnp.bfloat16),
            pltpu.VMEM((heads, total, dim), jnp.bfloat16),
            pltpu.VMEM((heads, width, text_rows), jnp.bfloat16),
            pltpu.SemaphoreType.DMA((len(kv), 2)),
            pltpu.SemaphoreType.DMA((3 + len(done),)),
            pltpu.SemaphoreType.DMA((STORES,)),
        ],
        compiler_params=pltpu.CompilerParams(vmem_limit_bytes=MIDDLE_VMEM),
        cost_estimate=lasting(5 * heads),
    )(home.reshape(1), tokens, hull, *kv, *done, q, hidden, back)


def shards(vision_states, kv_weight, key_gain, queries, tile_tokens, text_tiles):
    dim = key_gain.shape[0]
    all_heads = kv_weight.shape[1] // (2 * dim)
    tensor, segment, seq = lax.axis_size("tensor"), lax.axis_size("segment"), lax.axis_size("seq")
    heads = all_heads // tensor
    tiles = tile_tokens.shape[0]
    tile_len = vision_states.shape[0] * segment * seq // tiles
    if tensor == 2 and segment == 2 and seq == 8 and heads % CHUNKS == 0:
        return by_chunks(vision_states, kv_weight, key_gain, queries, tile_tokens, text_tiles, heads, tile_len)
    text = sort_rows(queries, text_tiles, tiles, dim)
    weight_heads = kv_weight.reshape(kv_weight.shape[0], all_heads, 2 * dim)
    partial = jnp.einsum("rd,dch->crh", vision_states, weight_heads, preferred_element_type=jnp.float32)
    sums = lax.psum_scatter(partial, "tensor", scatter_dimension=0, tiled=True)
    keys = sums[:, :, :dim]
    mean_sq = jnp.mean(keys * keys, axis=-1, keepdims=True)
    keys = keys * lax.rsqrt(mean_sq + 1e-05) * key_gain
    block = jnp.concatenate([keys, sums[:, :, dim:]], axis=-1).astype(jnp.bfloat16)
    kv = [lax.all_gather(block, ("segment", "seq"), axis=1, tiled=True)]
    return attend(text, 0, kv, [0], jnp.int32(0), tile_tokens, tile_len, [], True)


def after(first, then):
    return lax.optimization_barrier((first, then))[1]


def by_chunks(vision_states, kv_weight, key_gain, queries, tile_tokens, text_tiles, heads, tile_len):
    dim = key_gain.shape[0]
    me_tensor, me_segment, me_seq = lax.axis_index("tensor"), lax.axis_index("segment"), lax.axis_index("seq")
    count = heads // CHUNKS

    def across(array, axis, step):
        return lax.ppermute(array, axis, [(i, i ^ step) for i in range(lax.axis_size(axis))])

    def parts(*wanted):
        blocks = [(owner * CHUNKS + chunk).astype(jnp.int32) for owner, chunk in wanted]
        return project(vision_states, kv_weight, blocks, count * 2 * dim)

    text = sort_rows(queries, text_tiles, tile_tokens.shape[0], dim)
    home = me_segment * 8 + me_seq
    offsets = [8 * side + 2 * far + core for core in range(2) for side in range(2) for far in range(4)]
    other = 1 - me_tensor
    (theirs,) = parts((other, 0))
    arrived = [across(theirs, "tensor", 1)]
    rest = parts(*((other, chunk) for chunk in range(1, CHUNKS)), *((me_tensor, chunk) for chunk in range(CHUNKS)))
    arrived += [across(theirs, "tensor", 1) for theirs in rest[: CHUNKS - 1]]
    mine = rest[CHUNKS - 1 :]
    blocks = [finish(mine[chunk], arrived[chunk], key_gain, count, dim) for chunk in range(CHUNKS)]
    done = []
    for chunk, block in enumerate(blocks):
        last = chunk == CHUNKS - 1
        near, far = across(block, "seq", 2), across(block, "seq", 4)
        lane = [block, near, far, across(far, "seq", 2)]
        lane += [across(piece, "segment", 1) for piece in lane]
        if chunk == 0:
            lane[-2], text = lax.optimization_barrier((lane[-2], text))
        if done:
            lane[-1] = after(done[-1], lane[-1])
        kv = lane + [across(piece, "seq", 1) for piece in lane]
        done.append(attend(text, chunk * count, kv, offsets, home, tile_tokens, tile_len, done if last else [], last))
    return done[-1]


def solution(mesh):
    placed = (
        P(("segment", "seq"), "tensor"),
        P("tensor", None),
        P(),
        P("seq", "tensor", "segment"),
        P(),
        P("seq", None),
    )
    return jax.shard_map(
        shards, mesh=mesh, in_specs=placed, out_specs=P("seq", "tensor", "segment"), check_vma=False
    )
```

```python
import functools

import jax
import jax.numpy as jnp
from jax import lax
from jax.experimental import pallas as pl
from jax.experimental.pallas import tpu as pltpu
from jax.sharding import PartitionSpec as P

MASKED = -1e30
CHUNKS = 1
HALVES = 2
STORES = 2
LOG2E = 1.4426950408889634
BLOCK_ROWS = 128
LARGE_VMEM = 52 * 1024 * 1024
MIDDLE_VMEM = 44 * 1024 * 1024
SMALL_VMEM = 16 * 1024 * 1024
VMEM = pl.BlockSpec(memory_space=pltpu.VMEM)
SMEM = pl.BlockSpec(memory_space=pltpu.SMEM)
ANY = pl.BlockSpec(memory_space=pl.ANY)
HBM = pl.BlockSpec(memory_space=pltpu.HBM)
ROWS_BY_ROWS = (((1,), (1,)), ((), ()))
COLS_BY_COLS = (((0,), (0,)), ((), ()))


def lasting(microseconds):
    return pl.CostEstimate(flops=0, bytes_accessed=int(3.6e6 * microseconds), transcendentals=0)


def project_kernel(pieces, block_ref, vision_hbm_ref, weight_ref, *refs):
    count = block_ref.shape[0]
    out_hbm_refs, (vision_ref, held_ref, out_ref, vision_sem, sems, out_sems) = refs[:count], refs[count:]
    depth, cols = held_ref.shape[1:]
    load = pltpu.make_async_copy(vision_hbm_ref, vision_ref, vision_sem)
    load.start()
    copies = []
    for step in range(count * pieces):
        which, piece = divmod(step, pieces)
        across = pl.ds(pl.multiple_of(block_ref[which] * cols, cols), cols)
        copies.append(
            pltpu.make_async_copy(weight_ref.at[pl.ds(piece * depth, depth), across], held_ref.at[step], sems.at[step])
        )
        copies[-1].start()
    load.wait()
    stores = []
    for which in range(count):
        total = None
        for piece in range(pieces):
            copies[which * pieces + piece].wait()
            part = vision_ref[:, piece * depth : (piece + 1) * depth]
            product = jnp.dot(part, held_ref[which * pieces + piece], preferred_element_type=jnp.float32)
            total = product if piece == 0 else total + product
        out_ref[which] = total
        stores.append(pltpu.make_async_copy(out_ref.at[which], out_hbm_refs[which], out_sems.at[which]))
        stores[-1].start()
    for store in stores:
        store.wait()


def project(vision, weight, blocks, cols):
    rows, depth = vision.shape
    count = len(blocks)
    pieces = next(parts for parts in (5, 3, 2, 1) if depth % (parts * 128) == 0)
    return pl.pallas_call(
        functools.partial(project_kernel, pieces),
        in_specs=[SMEM, ANY, ANY],
        out_specs=[ANY] * count,
        out_shape=[jax.ShapeDtypeStruct((rows, cols), jnp.float32)] * count,
        scratch_shapes=[
            pltpu.VMEM((rows, depth), jnp.bfloat16),
            pltpu.VMEM((count * pieces, depth // pieces, cols), jnp.bfloat16),
            pltpu.VMEM((count, rows, cols), jnp.float32),
            pltpu.SemaphoreType.DMA,
            pltpu.SemaphoreType.DMA((count * pieces,)),
            pltpu.SemaphoreType.DMA((count,)),
        ],
        compiler_params=pltpu.CompilerParams(vmem_limit_bytes=LARGE_VMEM),
        cost_estimate=lasting(2 + 1.2 * count),
    )(jnp.stack(blocks), pltpu.with_memory_space_constraint(vision, pltpu.HBM), weight)


def finish_kernel(heads, dim, parts, own_ref, *refs):
    other_refs, gain_ref, out_ref = refs[:parts], refs[parts], refs[parts + 1]
    for head in range(heads):
        part, inside = divmod(head, heads // parts)
        at, other_at = head * 2 * dim, inside * 2 * dim
        keys = own_ref[:, at : at + dim] + other_refs[part][:, other_at : other_at + dim]
        mean_sq = jnp.mean(keys * keys, axis=-1, keepdims=True)
        keys = keys * lax.rsqrt(mean_sq + 1e-05) * gain_ref[...]
        values = own_ref[:, at + dim : at + 2 * dim] + other_refs[part][:, other_at + dim : other_at + 2 * dim]
        out_ref[head, :, :dim] = keys.astype(jnp.bfloat16)
        out_ref[head, :, dim:] = values.astype(jnp.bfloat16)


def finish(own, others, gain, heads, dim):
    rows = own.shape[0]
    return pl.pallas_call(
        functools.partial(finish_kernel, heads, dim, len(others)),
        in_specs=[VMEM] * (2 + len(others)),
        out_specs=VMEM,
        out_shape=jax.ShapeDtypeStruct((heads, rows, 2 * dim), jnp.bfloat16),
        compiler_params=pltpu.CompilerParams(vmem_limit_bytes=SMALL_VMEM),
        cost_estimate=lasting(1.5),
    )(own, *others, gain.reshape(1, dim))


def sort_kernel(tiles, group, q_ref, range_rows_ref, sorted_ref, hidden_ref, back_ref, hull_ref):
    rows, heads, width = q_ref.shape
    dim = width // group

    def order(lower, upper, at):
        key = jnp.where(upper > lower, (tiles - 1 - lower) * (tiles + 1) + tiles - upper, -1)
        return key * rows + at

    lower_row, upper_row = range_rows_ref[0:1, :], range_rows_ref[1:2, :]
    columns = jnp.concatenate([lower_row, upper_row] * 4, axis=0).astype(jnp.float32).T.astype(jnp.int32)
    lower, upper = columns[:, 0:1], columns[:, 1:2]
    order_col = order(lower, upper, lax.broadcasted_iota(jnp.int32, (rows, 1), 0))
    order_row = order(lower_row, upper_row, lax.broadcasted_iota(jnp.int32, (1, rows), 1))
    rank_row = jnp.sum(jnp.where(order_col < order_row, 1.0, 0.0), axis=0, keepdims=True).astype(jnp.int32)
    rank_col = jnp.sum(jnp.where(order_row < order_col, 1.0, 0.0), axis=1, keepdims=True).astype(jnp.int32)
    into = jnp.where(lax.broadcasted_iota(jnp.int32, (rows, rows), 0) == rank_row, 1.0, 0.0).astype(jnp.bfloat16)
    back = jnp.where(lax.broadcasted_iota(jnp.int32, (rows, rows), 1) == rank_col, 1.0, 0.0).astype(jnp.bfloat16)
    back_ref[...] = back
    seen_row = upper_row > lower_row
    blocks = rows // BLOCK_ROWS
    for block in range(blocks):
        inside = seen_row & (rank_row >= block * BLOCK_ROWS) & (rank_row < (block + 1) * BLOCK_ROWS)
        hull_ref[0, block] = jnp.min(jnp.where(inside, lower_row, tiles).astype(jnp.float32)).astype(jnp.int32)
        hull_ref[1, block] = jnp.max(jnp.where(inside, upper_row, 0).astype(jnp.float32)).astype(jnp.int32)
    hull_ref[2, 0] = jnp.sum(jnp.where(seen_row, 0.0, 1.0)).astype(jnp.int32)
    lanes = lax.broadcasted_iota(jnp.int32, (rows, dim), 1)
    unseen = (lanes < tiles) & ((lanes < lower) | (lanes >= upper)) | (lanes == tiles)
    hidden = jnp.where(unseen, 1.0, 0.0).astype(jnp.bfloat16)
    hidden_ref[...] = jnp.dot(into, hidden, preferred_element_type=jnp.float32).astype(jnp.bfloat16)
    q_heads = jnp.transpose(q_ref[...], (1, 0, 2))
    for head in range(heads):
        moved = jnp.dot(into, q_heads[head], preferred_element_type=jnp.float32).astype(jnp.bfloat16)
        for block in range(blocks):
            for member in range(group):
                at = (block * group + member) * BLOCK_ROWS
                sorted_ref[head, at : at + BLOCK_ROWS, :] = moved[
                    block * BLOCK_ROWS : (block + 1) * BLOCK_ROWS, member * dim : (member + 1) * dim
                ]


def sort_rows(queries, text_tiles, tiles, dim):
    rows, heads, width = queries.shape
    group = width // dim
    return pl.pallas_call(
        functools.partial(sort_kernel, tiles, group),
        in_specs=[VMEM, VMEM],
        out_specs=[VMEM, VMEM, VMEM, SMEM],
        out_shape=[
            jax.ShapeDtypeStruct((heads, rows * group, dim), jnp.bfloat16),
            jax.ShapeDtypeStruct((rows, dim), jnp.bfloat16),
            jax.ShapeDtypeStruct((rows, rows), jnp.bfloat16),
            jax.ShapeDtypeStruct((3, rows // BLOCK_ROWS), jnp.int32),
        ],
        compiler_params=pltpu.CompilerParams(vmem_limit_bytes=MIDDLE_VMEM),
        cost_estimate=lasting(5),
    )(queries, text_tiles.T)


def attend_kernel(shape, offsets, earlier, last, home_ref, tokens_ref, hull_ref, *refs):
    heads, first_head, blocks, group, dim, tiles, tile_len = shape
    pieces = len(offsets)
    kv_refs, refs = refs[:pieces], refs[pieces:]
    done_refs, refs = refs[:earlier], refs[earlier:]
    q_hbm_ref, hidden_hbm_ref, back_hbm_ref, result_hbm_ref = refs[:4]
    q_ref, hidden_ref, back_ref, done_ref, result_ref, k_ref, v_ref, turned_ref, sems, load_sems, store_sems = refs[4:]
    piece_rows = kv_refs[0].shape[1]
    columns = group * BLOCK_ROWS
    scale = LOG2E * dim ** (-0.5)
    copies = []
    for piece in range(pieces):
        at = pl.multiple_of((home_ref[0] ^ offsets[piece]) * piece_rows, piece_rows)
        into = k_ref.at[:, pl.ds(at, piece_rows), pl.ds(0, dim)], v_ref.at[:, pl.ds(at, piece_rows), :]
        for part in range(2):
            source = kv_refs[piece].at[:, :, pl.ds(part * dim, dim)]
            copies.append(pltpu.make_async_copy(source, into[part], sems.at[piece, part]))
            copies[-1].start()
    loads = [(q_hbm_ref.at[pl.ds(first_head, heads)], q_ref), (hidden_hbm_ref, hidden_ref), (back_hbm_ref, back_ref)]
    loads += [(ref, done_ref.at[pl.ds(i * heads, heads)]) for i, ref in enumerate(done_refs)]
    loads = [pltpu.make_async_copy(*ends, load_sems.at[i]) for i, ends in enumerate(loads)]
    for load in loads:
        load.start()
    lanes = lax.broadcasted_iota(jnp.int32, (tile_len, dim), 1)
    place = lax.broadcasted_iota(jnp.int32, (tile_len, dim), 0)
    for tile in range(tiles):
        off = (lanes == tile) | ((lanes == tiles) & (place >= tokens_ref[tile]))
        off = jnp.where(off, MASKED, 0.0).astype(jnp.bfloat16)
        for head in range(heads):
            k_ref[head, tile * tile_len : (tile + 1) * tile_len, dim:] = off
    for copy in [*copies, *loads[:2]]:
        copy.wait()

    def work(block, first, count):
        here = pl.ds(pl.multiple_of(block * BLOCK_ROWS, BLOCK_ROWS), BLOCK_ROWS)
        if count == 0:
            turned_ref[:, :, here] = jnp.zeros((heads, group * dim, BLOCK_ROWS), jnp.bfloat16)
            return
        rows = pl.ds(pl.multiple_of(block * columns, columns), columns)
        span = pl.ds(pl.multiple_of(first * tile_len, tile_len), count * tile_len)
        hidden = jnp.concatenate([hidden_ref[here, :]] * group, axis=0)
        row = lax.broadcasted_iota(jnp.int32, (1, columns), 1) % BLOCK_ROWS + block * BLOCK_ROWS
        scores = [
            lax.dot_general(
                k_ref[head, span, :],
                jnp.concatenate([q_ref[head, rows, :], hidden], axis=1),
                ROWS_BY_ROWS,
                preferred_element_type=jnp.float32,
            )
            for head in range(heads)
        ]
        for head in range(heads):
            row_max = jnp.max(scores[head], axis=0, keepdims=True)
            terms = jnp.exp2((scores[head] - row_max) * scale)
            denominator = jnp.sum(terms, axis=0, keepdims=True)
            summed = lax.dot_general(
                v_ref[head, span, :], terms.astype(jnp.bfloat16), COLS_BY_COLS, preferred_element_type=jnp.float32
            )
            inverse = jnp.where(row >= hull_ref[2, 0], 1.0 / denominator, 0.0)
            attended = (summed * inverse).astype(jnp.bfloat16)
            for member in range(group):
                turned_ref[head, member * dim : (member + 1) * dim, here] = attended[
                    :, member * BLOCK_ROWS : (member + 1) * BLOCK_ROWS
                ]

    @pl.loop(0, blocks)
    def _(block):
        first = hull_ref[0, block]
        seen = jnp.maximum(hull_ref[1, block] - first, 0)
        for count in range(tiles + 1):

            @pl.when(seen == count)
            def _():
                work(block, first, count)

    for load in loads[2:]:
        load.wait()
    if not last:
        store = pltpu.make_async_copy(turned_ref, result_hbm_ref, store_sems.at[0])
        store.start()
        store.wait()
        return
    stores = []
    rows = back_ref.shape[0] // STORES
    for part in range(STORES):
        here = pl.ds(part * rows, rows)
        back = back_ref[here, :]
        whole = [
            lax.dot_general(back, turned, ROWS_BY_ROWS, preferred_element_type=jnp.float32).astype(jnp.bfloat16)
            for turned in [done_ref[i] for i in range(first_head)] + [turned_ref[head] for head in range(heads)]
        ]
        result_ref[here] = jnp.transpose(jnp.stack(whole, axis=0), (1, 0, 2))
        stores.append(pltpu.make_async_copy(result_ref.at[here], result_hbm_ref.at[here], store_sems.at[part]))
        stores[-1].start()
    for store in stores:
        store.wait()


def attend(text, first, kv, offsets, home, tokens, tile_len, done, last):
    q, hidden, back, hull = text
    heads, dim = kv[0].shape[0], kv[0].shape[2] // 2
    text_rows, blocks = back.shape[0], hull.shape[1]
    group, tiles = q.shape[1] // text_rows, tokens.shape[0]
    width = group * dim
    total = sum(piece.shape[1] for piece in kv)
    whole = (text_rows, q.shape[0], width) if last else (heads, width, text_rows)
    return pl.pallas_call(
        functools.partial(attend_kernel, (heads, first, blocks, group, dim, tiles, tile_len), offsets, len(done), last),
        in_specs=[SMEM] * 3 + [ANY] * len(kv) + [HBM] * (len(done) + 3),
        out_specs=ANY,
        out_shape=jax.ShapeDtypeStruct(whole, jnp.bfloat16),
        scratch_shapes=[
            pltpu.VMEM((heads, *q.shape[1:]), jnp.bfloat16),
            pltpu.VMEM(hidden.shape, jnp.bfloat16),
            pltpu.VMEM(back.shape, jnp.bfloat16),
            pltpu.VMEM((max(first, 1), width, text_rows), jnp.bfloat16),
            pltpu.VMEM((text_rows, q.shape[0], width) if last else (8, 128), jnp.bfloat16),
            pltpu.VMEM((heads, total, 2 * dim), jnp.bfloat16),
            pltpu.VMEM((heads, total, dim), jnp.bfloat16),
            pltpu.VMEM((heads, width, text_rows), jnp.bfloat16),
            pltpu.SemaphoreType.DMA((len(kv), 2)),
            pltpu.SemaphoreType.DMA((3 + len(done),)),
            pltpu.SemaphoreType.DMA((STORES,)),
        ],
        compiler_params=pltpu.CompilerParams(vmem_limit_bytes=MIDDLE_VMEM),
        cost_estimate=lasting(5 * heads),
    )(home.reshape(1), tokens, hull, *(pltpu.with_memory_space_constraint(piece, pltpu.HBM) for piece in kv), *done, q, hidden, back)


def shards(vision_states, kv_weight, key_gain, queries, tile_tokens, text_tiles):
    dim = key_gain.shape[0]
    all_heads = kv_weight.shape[1] // (2 * dim)
    tensor, segment, seq = lax.axis_size("tensor"), lax.axis_size("segment"), lax.axis_size("seq")
    heads = all_heads // tensor
    tiles = tile_tokens.shape[0]
    tile_len = vision_states.shape[0] * segment * seq // tiles
    if tensor == 2 and segment == 2 and seq == 8 and heads % CHUNKS == 0:
        return by_chunks(vision_states, kv_weight, key_gain, queries, tile_tokens, text_tiles, heads, tile_len)
    text = sort_rows(queries, text_tiles, tiles, dim)
    weight_heads = kv_weight.reshape(kv_weight.shape[0], all_heads, 2 * dim)
    partial = jnp.einsum("rd,dch->crh", vision_states, weight_heads, preferred_element_type=jnp.float32)
    sums = lax.psum_scatter(partial, "tensor", scatter_dimension=0, tiled=True)
    keys = sums[:, :, :dim]
    mean_sq = jnp.mean(keys * keys, axis=-1, keepdims=True)
    keys = keys * lax.rsqrt(mean_sq + 1e-05) * key_gain
    block = jnp.concatenate([keys, sums[:, :, dim:]], axis=-1).astype(jnp.bfloat16)
    kv = [lax.all_gather(block, ("segment", "seq"), axis=1, tiled=True)]
    return attend(text, 0, kv, [0], jnp.int32(0), tile_tokens, tile_len, [], True)


def after(first, then):
    return lax.optimization_barrier((first, then))[1]


def by_chunks(vision_states, kv_weight, key_gain, queries, tile_tokens, text_tiles, heads, tile_len):
    dim = key_gain.shape[0]
    me_tensor, me_segment, me_seq = lax.axis_index("tensor"), lax.axis_index("segment"), lax.axis_index("seq")
    count = heads // CHUNKS

    def across(array, axis, step):
        return lax.ppermute(array, axis, [(i, i ^ step) for i in range(lax.axis_size(axis))])

    def parts(count, *blocks):
        return project(vision_states, kv_weight, [block.astype(jnp.int32) for block in blocks], heads * 2 * dim // count)

    text = sort_rows(queries, text_tiles, tile_tokens.shape[0], dim)
    home = me_segment * 8 + me_seq
    offsets = [8 * side + 2 * far + core for core in range(2) for side in range(2) for far in range(4)]
    other = 1 - me_tensor
    theirs = [parts(HALVES, other * HALVES + half)[0] for half in range(HALVES)]
    arrived = [across(half, "tensor", 1) for half in theirs]
    (mine,) = parts(1, me_tensor)
    blocks = [finish(mine, arrived, key_gain, count, dim)]
    done = []
    for chunk, block in enumerate(blocks):
        last = chunk == CHUNKS - 1
        near, far = across(block, "seq", 2), across(block, "seq", 4)
        lane = [block, near, far, across(far, "seq", 2)]
        lane += [across(piece, "segment", 1) for piece in lane]
        if chunk == 0:
            lane[-2], text = lax.optimization_barrier((lane[-2], text))
        if done:
            lane[-1] = after(done[-1], lane[-1])
        kv = lane + [across(piece, "seq", 1) for piece in lane]
        done.append(attend(text, chunk * count, kv, offsets, home, tile_tokens, tile_len, done if last else [], last))
    return done[-1]


def solution(mesh):
    placed = (
        P(("segment", "seq"), "tensor"),
        P("tensor", None),
        P(),
        P("seq", "tensor", "segment"),
        P(),
        P("seq", None),
    )
    return jax.shard_map(
        shards, mesh=mesh, in_specs=placed, out_specs=P("seq", "tensor", "segment"), check_vma=False
    )
```

```python
import functools

import jax
import jax.numpy as jnp
from jax import lax
from jax.experimental import pallas as pl
from jax.experimental.pallas import tpu as pltpu
from jax.sharding import PartitionSpec as P

MASKED = -1e30
HALVES = 2
STORES = 2
LOG2E = 1.4426950408889634
BLOCK_ROWS = 128
LARGE_VMEM = 52 * 1024 * 1024
MIDDLE_VMEM = 44 * 1024 * 1024
SMALL_VMEM = 16 * 1024 * 1024
VMEM = pl.BlockSpec(memory_space=pltpu.VMEM)
SMEM = pl.BlockSpec(memory_space=pltpu.SMEM)
ANY = pl.BlockSpec(memory_space=pl.ANY)
HBM = pl.BlockSpec(memory_space=pltpu.HBM)
ROWS_BY_ROWS = (((1,), (1,)), ((), ()))
COLS_BY_COLS = (((0,), (0,)), ((), ()))


def lasting(microseconds):
    return pl.CostEstimate(flops=0, bytes_accessed=int(3.6e6 * microseconds), transcendentals=0)


def project_kernel(pieces, block_ref, vision_hbm_ref, weight_ref, *refs):
    count = block_ref.shape[0]
    out_hbm_refs, (vision_ref, held_ref, out_ref, vision_sem, sems, out_sems) = refs[:count], refs[count:]
    depth, cols = held_ref.shape[1:]
    load = pltpu.make_async_copy(vision_hbm_ref, vision_ref, vision_sem)
    load.start()
    copies = []
    for step in range(count * pieces):
        which, piece = divmod(step, pieces)
        across = pl.ds(pl.multiple_of(block_ref[which] * cols, cols), cols)
        copies.append(
            pltpu.make_async_copy(weight_ref.at[pl.ds(piece * depth, depth), across], held_ref.at[step], sems.at[step])
        )
        copies[-1].start()
    load.wait()
    stores = []
    for which in range(count):
        total = None
        for piece in range(pieces):
            copies[which * pieces + piece].wait()
            part = vision_ref[:, piece * depth : (piece + 1) * depth]
            product = jnp.dot(part, held_ref[which * pieces + piece], preferred_element_type=jnp.float32)
            total = product if piece == 0 else total + product
        out_ref[which] = total
        stores.append(pltpu.make_async_copy(out_ref.at[which], out_hbm_refs[which], out_sems.at[which]))
        stores[-1].start()
    for store in stores:
        store.wait()


def project(vision, weight, blocks, cols):
    rows, depth = vision.shape
    count = len(blocks)
    pieces = next(parts for parts in (5, 3, 2, 1) if depth % (parts * 128) == 0)
    return pl.pallas_call(
        functools.partial(project_kernel, pieces),
        in_specs=[SMEM, ANY, ANY],
        out_specs=[ANY] * count,
        out_shape=[jax.ShapeDtypeStruct((rows, cols), jnp.float32)] * count,
        scratch_shapes=[
            pltpu.VMEM((rows, depth), jnp.bfloat16),
            pltpu.VMEM((count * pieces, depth // pieces, cols), jnp.bfloat16),
            pltpu.VMEM((count, rows, cols), jnp.float32),
            pltpu.SemaphoreType.DMA,
            pltpu.SemaphoreType.DMA((count * pieces,)),
            pltpu.SemaphoreType.DMA((count,)),
        ],
        compiler_params=pltpu.CompilerParams(vmem_limit_bytes=LARGE_VMEM),
        cost_estimate=lasting(2 + 1.2 * count),
    )(jnp.stack(blocks), pltpu.with_memory_space_constraint(vision, pltpu.HBM), weight)


def finish_kernel(heads, dim, parts, own_ref, *refs):
    other_refs, gain_ref, out_ref = refs[:parts], refs[parts], refs[parts + 1]
    for head in range(heads):
        part, inside = divmod(head, heads // parts)
        at, other_at = head * 2 * dim, inside * 2 * dim
        keys = own_ref[:, at : at + dim] + other_refs[part][:, other_at : other_at + dim]
        mean_sq = jnp.mean(keys * keys, axis=-1, keepdims=True)
        keys = keys * lax.rsqrt(mean_sq + 1e-05) * gain_ref[...]
        values = own_ref[:, at + dim : at + 2 * dim] + other_refs[part][:, other_at + dim : other_at + 2 * dim]
        out_ref[head, :, :dim] = keys.astype(jnp.bfloat16)
        out_ref[head, :, dim:] = values.astype(jnp.bfloat16)


def finish(own, others, gain, heads, dim):
    rows = own.shape[0]
    return pl.pallas_call(
        functools.partial(finish_kernel, heads, dim, len(others)),
        in_specs=[VMEM] * (2 + len(others)),
        out_specs=VMEM,
        out_shape=jax.ShapeDtypeStruct((heads, rows, 2 * dim), jnp.bfloat16),
        compiler_params=pltpu.CompilerParams(vmem_limit_bytes=SMALL_VMEM),
        cost_estimate=lasting(1.5),
    )(own, *others, gain.reshape(1, dim))


def sort_kernel(tiles, group, q_ref, range_rows_ref, sorted_ref, hidden_ref, back_ref, hull_ref):
    rows, heads, width = q_ref.shape
    dim = width // group

    def order(lower, upper, at):
        key = jnp.where(upper > lower, (tiles - 1 - lower) * (tiles + 1) + tiles - upper, -1)
        return key * rows + at

    lower_row, upper_row = range_rows_ref[0:1, :], range_rows_ref[1:2, :]
    columns = jnp.concatenate([lower_row, upper_row] * 4, axis=0).astype(jnp.float32).T.astype(jnp.int32)
    lower, upper = columns[:, 0:1], columns[:, 1:2]
    order_col = order(lower, upper, lax.broadcasted_iota(jnp.int32, (rows, 1), 0))
    order_row = order(lower_row, upper_row, lax.broadcasted_iota(jnp.int32, (1, rows), 1))
    rank_row = jnp.sum(jnp.where(order_col < order_row, 1.0, 0.0), axis=0, keepdims=True).astype(jnp.int32)
    rank_col = jnp.sum(jnp.where(order_row < order_col, 1.0, 0.0), axis=1, keepdims=True).astype(jnp.int32)
    into = jnp.where(lax.broadcasted_iota(jnp.int32, (rows, rows), 0) == rank_row, 1.0, 0.0).astype(jnp.bfloat16)
    back = jnp.where(lax.broadcasted_iota(jnp.int32, (rows, rows), 1) == rank_col, 1.0, 0.0).astype(jnp.bfloat16)
    back_ref[...] = back
    seen_row = upper_row > lower_row
    blocks = rows // BLOCK_ROWS
    for block in range(blocks):
        inside = seen_row & (rank_row >= block * BLOCK_ROWS) & (rank_row < (block + 1) * BLOCK_ROWS)
        hull_ref[0, block] = jnp.min(jnp.where(inside, lower_row, tiles).astype(jnp.float32)).astype(jnp.int32)
        hull_ref[1, block] = jnp.max(jnp.where(inside, upper_row, 0).astype(jnp.float32)).astype(jnp.int32)
    hull_ref[2, 0] = jnp.sum(jnp.where(seen_row, 0.0, 1.0)).astype(jnp.int32)
    lanes = lax.broadcasted_iota(jnp.int32, (rows, dim), 1)
    unseen = (lanes < tiles) & ((lanes < lower) | (lanes >= upper)) | (lanes == tiles)
    hidden = jnp.where(unseen, 1.0, 0.0).astype(jnp.bfloat16)
    hidden_ref[...] = jnp.dot(into, hidden, preferred_element_type=jnp.float32).astype(jnp.bfloat16)
    q_heads = jnp.transpose(q_ref[...], (1, 0, 2))
    for head in range(heads):
        moved = jnp.dot(into, q_heads[head], preferred_element_type=jnp.float32).astype(jnp.bfloat16)
        for block in range(blocks):
            for member in range(group):
                at = (block * group + member) * BLOCK_ROWS
                sorted_ref[head, at : at + BLOCK_ROWS, :] = moved[
                    block * BLOCK_ROWS : (block + 1) * BLOCK_ROWS, member * dim : (member + 1) * dim
                ]


def sort_rows(queries, text_tiles, tiles, dim):
    rows, heads, width = queries.shape
    group = width // dim
    return pl.pallas_call(
        functools.partial(sort_kernel, tiles, group),
        in_specs=[VMEM, VMEM],
        out_specs=[VMEM, VMEM, VMEM, SMEM],
        out_shape=[
            jax.ShapeDtypeStruct((heads, rows * group, dim), jnp.bfloat16),
            jax.ShapeDtypeStruct((rows, dim), jnp.bfloat16),
            jax.ShapeDtypeStruct((rows, rows), jnp.bfloat16),
            jax.ShapeDtypeStruct((3, rows // BLOCK_ROWS), jnp.int32),
        ],
        compiler_params=pltpu.CompilerParams(vmem_limit_bytes=MIDDLE_VMEM),
        cost_estimate=lasting(0.1),
    )(queries, text_tiles.T)


def attend_kernel(shape, offsets, home_ref, tokens_ref, hull_ref, *refs):
    heads, blocks, group, dim, tiles, tile_len = shape
    pieces = len(offsets)
    piece_refs, refs = refs[:pieces], refs[pieces:]
    q_ref, hidden_ref, back_ref, result_hbm_ref, kv_ref, off_ref, turned_ref, result_ref, load_sems, store_sems = refs
    piece_rows = piece_refs[0].shape[1]
    columns = group * BLOCK_ROWS
    scale = LOG2E * dim ** (-0.5)
    loads = []
    for piece in range(pieces):
        at = pl.multiple_of((home_ref[0] ^ offsets[piece]) * piece_rows, piece_rows)
        loads.append(pltpu.make_async_copy(piece_refs[piece], kv_ref.at[:, pl.ds(at, piece_rows), :], load_sems.at[piece]))
        loads[-1].start()
    lanes = lax.broadcasted_iota(jnp.int32, (tile_len, dim), 1)
    place = lax.broadcasted_iota(jnp.int32, (tile_len, dim), 0)
    for tile in range(tiles):
        off = (lanes == tile) | ((lanes == tiles) & (place >= tokens_ref[tile]))
        off_ref[tile * tile_len : (tile + 1) * tile_len, :] = jnp.where(off, MASKED, 0.0).astype(jnp.bfloat16)
    for load in loads:
        load.wait()

    def work(block, first, count):
        here = pl.ds(pl.multiple_of(block * BLOCK_ROWS, BLOCK_ROWS), BLOCK_ROWS)
        if count == 0:
            turned_ref[:, :, here] = jnp.zeros((heads, group * dim, BLOCK_ROWS), jnp.bfloat16)
            return
        rows = pl.ds(pl.multiple_of(block * columns, columns), columns)
        span = pl.ds(pl.multiple_of(first * tile_len, tile_len), count * tile_len)
        hidden = jnp.concatenate([hidden_ref[here, :]] * group, axis=0)
        off = off_ref[span, :]
        row = lax.broadcasted_iota(jnp.int32, (1, columns), 1) % BLOCK_ROWS + block * BLOCK_ROWS
        scores = [
            lax.dot_general(
                jnp.concatenate([kv_ref[head, span, :dim], off], axis=1),
                jnp.concatenate([q_ref[head, rows, :], hidden], axis=1),
                ROWS_BY_ROWS,
                preferred_element_type=jnp.float32,
            )
            for head in range(heads)
        ]
        for head in range(heads):
            row_max = jnp.max(scores[head], axis=0, keepdims=True)
            terms = jnp.exp2((scores[head] - row_max) * scale)
            total = jnp.sum(terms, axis=0, keepdims=True)
            summed = lax.dot_general(
                kv_ref[head, span, dim:], terms.astype(jnp.bfloat16), COLS_BY_COLS, preferred_element_type=jnp.float32
            )
            inverse = jnp.where(row >= hull_ref[2, 0], 1.0 / total, 0.0)
            attended = (summed * inverse).astype(jnp.bfloat16)
            for member in range(group):
                turned_ref[head, member * dim : (member + 1) * dim, here] = attended[
                    :, member * BLOCK_ROWS : (member + 1) * BLOCK_ROWS
                ]

    @pl.loop(0, blocks)
    def _(block):
        first = hull_ref[0, block]
        seen = jnp.maximum(hull_ref[1, block] - first, 0)
        for count in range(tiles + 1):

            @pl.when(seen == count)
            def _():
                work(block, first, count)

    stores = []
    rows = back_ref.shape[0] // STORES
    for part in range(STORES):
        here = pl.ds(part * rows, rows)
        back = back_ref[here, :]
        whole = [
            lax.dot_general(back, turned_ref[head], ROWS_BY_ROWS, preferred_element_type=jnp.float32)
            for head in range(heads)
        ]
        whole = jnp.stack([head.astype(jnp.bfloat16) for head in whole], axis=0)
        result_ref[here] = jnp.transpose(whole, (1, 0, 2))
        stores.append(pltpu.make_async_copy(result_ref.at[here], result_hbm_ref.at[here], store_sems.at[part]))
        stores[-1].start()
    for store in stores:
        store.wait()


def attend(text, kv, offsets, home, tokens, tile_len):
    q, hidden, back, hull = text
    heads, dim = kv[0].shape[0], kv[0].shape[2] // 2
    text_rows, blocks = back.shape[0], hull.shape[1]
    group, tiles = q.shape[1] // text_rows, tokens.shape[0]
    width = group * dim
    total = sum(piece.shape[1] for piece in kv)
    kv = [pltpu.with_memory_space_constraint(piece, pltpu.HBM) for piece in kv]
    return pl.pallas_call(
        functools.partial(attend_kernel, (heads, blocks, group, dim, tiles, tile_len), offsets),
        in_specs=[SMEM] * 3 + [ANY] * len(kv) + [VMEM] * 3,
        out_specs=ANY,
        out_shape=jax.ShapeDtypeStruct((text_rows, heads, width), jnp.bfloat16),
        scratch_shapes=[
            pltpu.VMEM((heads, total, 2 * dim), jnp.bfloat16),
            pltpu.VMEM((total, dim), jnp.bfloat16),
            pltpu.VMEM((heads, width, text_rows), jnp.bfloat16),
            pltpu.VMEM((text_rows, heads, width), jnp.bfloat16),
            pltpu.SemaphoreType.DMA((len(kv),)),
            pltpu.SemaphoreType.DMA((STORES,)),
        ],
        compiler_params=pltpu.CompilerParams(vmem_limit_bytes=MIDDLE_VMEM),
        cost_estimate=lasting(15),
    )(home.reshape(1), tokens, hull, *kv, q, hidden, back)


def shards(vision_states, kv_weight, key_gain, queries, tile_tokens, text_tiles):
    dim = key_gain.shape[0]
    all_heads = kv_weight.shape[1] // (2 * dim)
    tensor, segment, seq = lax.axis_size("tensor"), lax.axis_size("segment"), lax.axis_size("seq")
    heads = all_heads // tensor
    tiles = tile_tokens.shape[0]
    tile_len = vision_states.shape[0] * segment * seq // tiles
    if tensor == 2 and segment == 2 and seq == 8 and heads % HALVES == 0:
        return by_swaps(vision_states, kv_weight, key_gain, queries, tile_tokens, text_tiles, heads, tile_len)
    text = sort_rows(queries, text_tiles, tiles, dim)
    weight_heads = kv_weight.reshape(kv_weight.shape[0], all_heads, 2 * dim)
    partial = jnp.einsum("rd,dch->crh", vision_states, weight_heads, preferred_element_type=jnp.float32)
    sums = lax.psum_scatter(partial, "tensor", scatter_dimension=0, tiled=True)
    keys = sums[:, :, :dim]
    mean_sq = jnp.mean(keys * keys, axis=-1, keepdims=True)
    keys = keys * lax.rsqrt(mean_sq + 1e-05) * key_gain
    block = jnp.concatenate([keys, sums[:, :, dim:]], axis=-1).astype(jnp.bfloat16)
    kv = [lax.all_gather(block, ("segment", "seq"), axis=1, tiled=True)]
    return attend(text, kv, [0], jnp.int32(0), tile_tokens, tile_len)


def after(first, then):
    return lax.optimization_barrier((first, then))[1]


def by_swaps(vision_states, kv_weight, key_gain, queries, tile_tokens, text_tiles, heads, tile_len):
    dim = key_gain.shape[0]
    me_tensor, me_segment, me_seq = lax.axis_index("tensor"), lax.axis_index("segment"), lax.axis_index("seq")

    def across(array, axis, step):
        return lax.ppermute(array, axis, [(i, i ^ step) for i in range(lax.axis_size(axis))])

    def parts(count, *blocks):
        return project(vision_states, kv_weight, [block.astype(jnp.int32) for block in blocks], heads * 2 * dim // count)

    text = sort_rows(queries, text_tiles, tile_tokens.shape[0], dim)
    home = me_segment * 8 + me_seq
    offsets = [8 * side + 2 * far + core for core in range(2) for side in range(2) for far in range(4)]
    other = 1 - me_tensor
    theirs = [parts(HALVES, other * HALVES + half)[0] for half in range(HALVES)]
    arrived = [across(half, "tensor", 1) for half in theirs]
    (mine,) = parts(1, me_tensor)
    block = finish(mine, arrived, key_gain, heads, dim)
    near, far, side = across(block, "seq", 2), across(block, "seq", 4), across(block, "segment", 1)
    far_near, side_far = across(far, "seq", 2), across(far, "segment", 1)
    side_near = across(after(far_near, side), "seq", 2)
    side_far, text = lax.optimization_barrier((side_far, text))
    lane = [block, near, far, far_near, side, side_near, side_far, across(far_near, "segment", 1)]
    kv = lane + [across(piece, "seq", 1) for piece in lane]
    return attend(text, kv, offsets, home, tile_tokens, tile_len)


def solution(mesh):
    placed = (
        P(("segment", "seq"), "tensor"),
        P("tensor", None),
        P(),
        P("seq", "tensor", "segment"),
        P(),
        P("seq", None),
    )
    return jax.shard_map(
        shards, mesh=mesh, in_specs=placed, out_specs=P("seq", "tensor", "segment"), check_vma=False
    )
```

```python
import functools

import jax
import jax.numpy as jnp
from jax import lax
from jax.experimental import pallas as pl
from jax.experimental.pallas import tpu as pltpu
from jax.sharding import PartitionSpec as P

MASKED = -1e30
HALVES = 2
STORES = 2
LOG2E = 1.4426950408889634
BLOCK_ROWS = 128
LARGE_VMEM = 52 * 1024 * 1024
MIDDLE_VMEM = 44 * 1024 * 1024
SMALL_VMEM = 16 * 1024 * 1024
VMEM = pl.BlockSpec(memory_space=pltpu.VMEM)
SMEM = pl.BlockSpec(memory_space=pltpu.SMEM)
ANY = pl.BlockSpec(memory_space=pl.ANY)
HBM = pl.BlockSpec(memory_space=pltpu.HBM)
ROWS_BY_ROWS = (((1,), (1,)), ((), ()))
COLS_BY_COLS = (((0,), (0,)), ((), ()))


def lasting(microseconds):
    return pl.CostEstimate(flops=0, bytes_accessed=int(3.6e6 * microseconds), transcendentals=0)


def project_kernel(pieces, block_ref, vision_hbm_ref, weight_ref, *refs):
    count = block_ref.shape[0]
    out_hbm_refs, (vision_ref, held_ref, out_ref, vision_sem, sems, out_sems) = refs[:count], refs[count:]
    depth, cols = held_ref.shape[1:]
    load = pltpu.make_async_copy(vision_hbm_ref, vision_ref, vision_sem)
    load.start()
    copies = []
    for step in range(count * pieces):
        which, piece = divmod(step, pieces)
        across = pl.ds(pl.multiple_of(block_ref[which] * cols, cols), cols)
        copies.append(
            pltpu.make_async_copy(weight_ref.at[pl.ds(piece * depth, depth), across], held_ref.at[step], sems.at[step])
        )
        copies[-1].start()
    load.wait()
    stores = []
    for which in range(count):
        total = None
        for piece in range(pieces):
            copies[which * pieces + piece].wait()
            part = vision_ref[:, piece * depth : (piece + 1) * depth]
            product = jnp.dot(part, held_ref[which * pieces + piece], preferred_element_type=jnp.float32)
            total = product if piece == 0 else total + product
        out_ref[which] = total
        stores.append(pltpu.make_async_copy(out_ref.at[which], out_hbm_refs[which], out_sems.at[which]))
        stores[-1].start()
    for store in stores:
        store.wait()


def project(vision, weight, blocks, cols):
    rows, depth = vision.shape
    count = len(blocks)
    pieces = next(parts for parts in (5, 3, 2, 1) if depth % (parts * 128) == 0)
    return pl.pallas_call(
        functools.partial(project_kernel, pieces),
        in_specs=[SMEM, ANY, ANY],
        out_specs=[ANY] * count,
        out_shape=[jax.ShapeDtypeStruct((rows, cols), jnp.float32)] * count,
        scratch_shapes=[
            pltpu.VMEM((rows, depth), jnp.bfloat16),
            pltpu.VMEM((count * pieces, depth // pieces, cols), jnp.bfloat16),
            pltpu.VMEM((count, rows, cols), jnp.float32),
            pltpu.SemaphoreType.DMA,
            pltpu.SemaphoreType.DMA((count * pieces,)),
            pltpu.SemaphoreType.DMA((count,)),
        ],
        compiler_params=pltpu.CompilerParams(vmem_limit_bytes=LARGE_VMEM),
        cost_estimate=lasting(2 + 1.2 * count),
    )(jnp.stack(blocks), pltpu.with_memory_space_constraint(vision, pltpu.HBM), weight)


def finish_kernel(heads, dim, parts, own_ref, *refs):
    other_refs, gain_ref, out_ref = refs[:parts], refs[parts], refs[parts + 1]
    for head in range(heads):
        part, inside = divmod(head, heads // parts)
        at, other_at = head * 2 * dim, inside * 2 * dim
        keys = own_ref[:, at : at + dim] + other_refs[part][:, other_at : other_at + dim]
        mean_sq = jnp.mean(keys * keys, axis=-1, keepdims=True)
        keys = keys * lax.rsqrt(mean_sq + 1e-05) * gain_ref[...]
        values = own_ref[:, at + dim : at + 2 * dim] + other_refs[part][:, other_at + dim : other_at + 2 * dim]
        out_ref[head, :, :dim] = keys.astype(jnp.bfloat16)
        out_ref[head, :, dim:] = values.astype(jnp.bfloat16)


def finish(own, others, gain, heads, dim):
    rows = own.shape[0]
    return pl.pallas_call(
        functools.partial(finish_kernel, heads, dim, len(others)),
        in_specs=[VMEM] * (2 + len(others)),
        out_specs=VMEM,
        out_shape=jax.ShapeDtypeStruct((heads, rows, 2 * dim), jnp.bfloat16),
        compiler_params=pltpu.CompilerParams(vmem_limit_bytes=SMALL_VMEM),
        cost_estimate=lasting(1.5),
    )(own, *others, gain.reshape(1, dim))


def sort_kernel(tiles, group, q_ref, range_rows_ref, sorted_ref, hidden_ref, back_ref, hull_ref):
    rows, heads, width = q_ref.shape
    dim = width // group

    def order(lower, upper, at):
        key = jnp.where(upper > lower, (tiles - 1 - lower) * (tiles + 1) + tiles - upper, -1)
        return key * rows + at

    lower_row, upper_row = range_rows_ref[0:1, :], range_rows_ref[1:2, :]
    columns = jnp.concatenate([lower_row, upper_row] * 4, axis=0).astype(jnp.float32).T.astype(jnp.int32)
    lower, upper = columns[:, 0:1], columns[:, 1:2]
    order_col = order(lower, upper, lax.broadcasted_iota(jnp.int32, (rows, 1), 0))
    order_row = order(lower_row, upper_row, lax.broadcasted_iota(jnp.int32, (1, rows), 1))
    rank_row = jnp.sum(jnp.where(order_col < order_row, 1.0, 0.0), axis=0, keepdims=True).astype(jnp.int32)
    rank_col = jnp.sum(jnp.where(order_row < order_col, 1.0, 0.0), axis=1, keepdims=True).astype(jnp.int32)
    into = jnp.where(lax.broadcasted_iota(jnp.int32, (rows, rows), 0) == rank_row, 1.0, 0.0).astype(jnp.bfloat16)
    back = jnp.where(lax.broadcasted_iota(jnp.int32, (rows, rows), 1) == rank_col, 1.0, 0.0).astype(jnp.bfloat16)
    back_ref[...] = back
    seen_row = upper_row > lower_row
    blocks = rows // BLOCK_ROWS
    for block in range(blocks):
        inside = seen_row & (rank_row >= block * BLOCK_ROWS) & (rank_row < (block + 1) * BLOCK_ROWS)
        hull_ref[0, block] = jnp.min(jnp.where(inside, lower_row, tiles).astype(jnp.float32)).astype(jnp.int32)
        hull_ref[1, block] = jnp.max(jnp.where(inside, upper_row, 0).astype(jnp.float32)).astype(jnp.int32)
    hull_ref[2, 0] = jnp.sum(jnp.where(seen_row, 0.0, 1.0)).astype(jnp.int32)
    lanes = lax.broadcasted_iota(jnp.int32, (rows, dim), 1)
    unseen = (lanes < tiles) & ((lanes < lower) | (lanes >= upper)) | (lanes == tiles)
    hidden = jnp.where(unseen, 1.0, 0.0).astype(jnp.bfloat16)
    hidden_ref[...] = jnp.dot(into, hidden, preferred_element_type=jnp.float32).astype(jnp.bfloat16)
    q_heads = jnp.transpose(q_ref[...], (1, 0, 2))
    for head in range(heads):
        moved = jnp.dot(into, q_heads[head], preferred_element_type=jnp.float32).astype(jnp.bfloat16)
        for block in range(blocks):
            for member in range(group):
                at = (block * group + member) * BLOCK_ROWS
                sorted_ref[head, at : at + BLOCK_ROWS, :] = moved[
                    block * BLOCK_ROWS : (block + 1) * BLOCK_ROWS, member * dim : (member + 1) * dim
                ]


def sort_rows(queries, text_tiles, tiles, dim):
    rows, heads, width = queries.shape
    group = width // dim
    return pl.pallas_call(
        functools.partial(sort_kernel, tiles, group),
        in_specs=[VMEM, VMEM],
        out_specs=[VMEM, VMEM, VMEM, SMEM],
        out_shape=[
            jax.ShapeDtypeStruct((heads, rows * group, dim), jnp.bfloat16),
            jax.ShapeDtypeStruct((rows, dim), jnp.bfloat16),
            jax.ShapeDtypeStruct((rows, rows), jnp.bfloat16),
            jax.ShapeDtypeStruct((3, rows // BLOCK_ROWS), jnp.int32),
        ],
        compiler_params=pltpu.CompilerParams(vmem_limit_bytes=MIDDLE_VMEM),
        cost_estimate=lasting(0.1),
    )(queries, text_tiles.T)


def attend_kernel(shape, offsets, home_ref, tokens_ref, hull_ref, *refs):
    heads, blocks, group, dim, tiles, tile_len = shape
    pieces = len(offsets)
    piece_refs, refs = refs[:pieces], refs[pieces:]
    q_ref, hidden_ref, back_ref, result_hbm_ref, kv_ref, off_ref, turned_ref, result_ref, load_sems, store_sems = refs
    piece_rows = piece_refs[0].shape[1]
    columns = group * BLOCK_ROWS
    scale = LOG2E * dim ** (-0.5)
    loads = []
    for piece in range(pieces):
        at = pl.multiple_of((home_ref[0] ^ offsets[piece]) * piece_rows, piece_rows)
        loads.append(pltpu.make_async_copy(piece_refs[piece], kv_ref.at[:, pl.ds(at, piece_rows), :], load_sems.at[piece]))
        loads[-1].start()
    lanes = lax.broadcasted_iota(jnp.int32, (tile_len, dim), 1)
    place = lax.broadcasted_iota(jnp.int32, (tile_len, dim), 0)
    for tile in range(tiles):
        off = (lanes == tile) | ((lanes == tiles) & (place >= tokens_ref[tile]))
        off_ref[tile * tile_len : (tile + 1) * tile_len, :] = jnp.where(off, MASKED, 0.0).astype(jnp.bfloat16)
    for load in loads:
        load.wait()

    def work(block, first, count):
        here = pl.ds(pl.multiple_of(block * BLOCK_ROWS, BLOCK_ROWS), BLOCK_ROWS)
        if count == 0:
            turned_ref[:, :, here] = jnp.zeros((heads, group * dim, BLOCK_ROWS), jnp.bfloat16)
            return
        rows = pl.ds(pl.multiple_of(block * columns, columns), columns)
        span = pl.ds(pl.multiple_of(first * tile_len, tile_len), count * tile_len)
        hidden = jnp.concatenate([hidden_ref[here, :]] * group, axis=0)
        off = off_ref[span, :]
        row = lax.broadcasted_iota(jnp.int32, (1, columns), 1) % BLOCK_ROWS + block * BLOCK_ROWS
        scores = [
            lax.dot_general(
                jnp.concatenate([kv_ref[head, span, :dim], off], axis=1),
                jnp.concatenate([q_ref[head, rows, :], hidden], axis=1),
                ROWS_BY_ROWS,
                preferred_element_type=jnp.float32,
            )
            for head in range(heads)
        ]
        for head in range(heads):
            row_max = jnp.max(scores[head], axis=0, keepdims=True)
            terms = jnp.exp2((scores[head] - row_max) * scale)
            total = jnp.sum(terms, axis=0, keepdims=True)
            summed = lax.dot_general(
                kv_ref[head, span, dim:], terms.astype(jnp.bfloat16), COLS_BY_COLS, preferred_element_type=jnp.float32
            )
            inverse = jnp.where(row >= hull_ref[2, 0], 1.0 / total, 0.0)
            attended = (summed * inverse).astype(jnp.bfloat16)
            for member in range(group):
                turned_ref[head, member * dim : (member + 1) * dim, here] = attended[
                    :, member * BLOCK_ROWS : (member + 1) * BLOCK_ROWS
                ]

    @pl.loop(0, blocks)
    def _(block):
        first = hull_ref[0, block]
        seen = jnp.maximum(hull_ref[1, block] - first, 0)
        for count in range(tiles + 1):

            @pl.when(seen == count)
            def _():
                work(block, first, count)

    stores = []
    rows = back_ref.shape[0] // STORES
    for part in range(STORES):
        here = pl.ds(part * rows, rows)
        back = back_ref[here, :]
        whole = [
            lax.dot_general(back, turned_ref[head], ROWS_BY_ROWS, preferred_element_type=jnp.float32)
            for head in range(heads)
        ]
        whole = jnp.stack([head.astype(jnp.bfloat16) for head in whole], axis=0)
        result_ref[here] = jnp.transpose(whole, (1, 0, 2))
        stores.append(pltpu.make_async_copy(result_ref.at[here], result_hbm_ref.at[here], store_sems.at[part]))
        stores[-1].start()
    for store in stores:
        store.wait()


def attend(text, kv, offsets, home, tokens, tile_len):
    q, hidden, back, hull = text
    heads, dim = kv[0].shape[0], kv[0].shape[2] // 2
    text_rows, blocks = back.shape[0], hull.shape[1]
    group, tiles = q.shape[1] // text_rows, tokens.shape[0]
    width = group * dim
    total = sum(piece.shape[1] for piece in kv)
    kv = [pltpu.with_memory_space_constraint(piece, pltpu.HBM) for piece in kv]
    return pl.pallas_call(
        functools.partial(attend_kernel, (heads, blocks, group, dim, tiles, tile_len), offsets),
        in_specs=[SMEM] * 3 + [ANY] * len(kv) + [VMEM] * 3,
        out_specs=ANY,
        out_shape=jax.ShapeDtypeStruct((text_rows, heads, width), jnp.bfloat16),
        scratch_shapes=[
            pltpu.VMEM((heads, total, 2 * dim), jnp.bfloat16),
            pltpu.VMEM((total, dim), jnp.bfloat16),
            pltpu.VMEM((heads, width, text_rows), jnp.bfloat16),
            pltpu.VMEM((text_rows, heads, width), jnp.bfloat16),
            pltpu.SemaphoreType.DMA((len(kv),)),
            pltpu.SemaphoreType.DMA((STORES,)),
        ],
        compiler_params=pltpu.CompilerParams(vmem_limit_bytes=MIDDLE_VMEM),
        cost_estimate=lasting(15),
    )(home.reshape(1), tokens, hull, *kv, q, hidden, back)


def shards(vision_states, kv_weight, key_gain, queries, tile_tokens, text_tiles):
    dim = key_gain.shape[0]
    all_heads = kv_weight.shape[1] // (2 * dim)
    tensor, segment, seq = lax.axis_size("tensor"), lax.axis_size("segment"), lax.axis_size("seq")
    heads = all_heads // tensor
    tiles = tile_tokens.shape[0]
    tile_len = vision_states.shape[0] * segment * seq // tiles
    if tensor == 2 and segment == 2 and seq == 8 and heads % HALVES == 0:
        return by_swaps(vision_states, kv_weight, key_gain, queries, tile_tokens, text_tiles, heads, tile_len)
    text = sort_rows(queries, text_tiles, tiles, dim)
    weight_heads = kv_weight.reshape(kv_weight.shape[0], all_heads, 2 * dim)
    partial = jnp.einsum("rd,dch->crh", vision_states, weight_heads, preferred_element_type=jnp.float32)
    sums = lax.psum_scatter(partial, "tensor", scatter_dimension=0, tiled=True)
    keys = sums[:, :, :dim]
    mean_sq = jnp.mean(keys * keys, axis=-1, keepdims=True)
    keys = keys * lax.rsqrt(mean_sq + 1e-05) * key_gain
    block = jnp.concatenate([keys, sums[:, :, dim:]], axis=-1).astype(jnp.bfloat16)
    kv = [lax.all_gather(block, ("segment", "seq"), axis=1, tiled=True)]
    return attend(text, kv, [0], jnp.int32(0), tile_tokens, tile_len)


def after(first, then):
    return lax.optimization_barrier((first, then))[1]


def by_swaps(vision_states, kv_weight, key_gain, queries, tile_tokens, text_tiles, heads, tile_len):
    dim = key_gain.shape[0]
    me_tensor, me_segment, me_seq = lax.axis_index("tensor"), lax.axis_index("segment"), lax.axis_index("seq")

    def across(array, axis, step):
        return lax.ppermute(array, axis, [(i, i ^ step) for i in range(lax.axis_size(axis))])

    def parts(count, *blocks):
        return project(vision_states, kv_weight, [block.astype(jnp.int32) for block in blocks], heads * 2 * dim // count)

    text = sort_rows(queries, text_tiles, tile_tokens.shape[0], dim)
    home = me_segment * 8 + me_seq
    offsets = [8 * side + 2 * far + core for core in range(2) for side in range(2) for far in range(4)]
    other = 1 - me_tensor
    theirs = [parts(HALVES, other * HALVES + half)[0] for half in range(HALVES)]
    arrived = [across(half, "tensor", 1) for half in theirs]
    (mine,) = parts(1, me_tensor)
    block = finish(mine, arrived, key_gain, heads, dim)
    near, far, side = across(block, "seq", 2), across(block, "seq", 4), across(after(text, block), "segment", 1)
    far_near, side_far = across(after(near, far), "seq", 2), across(far, "segment", 1)
    side_near = across(side, "seq", 2)
    lane = [block, near, far, far_near, side, side_near, side_far, across(far_near, "segment", 1)]
    kv = lane + [across(piece, "seq", 1) for piece in lane]
    return attend(text, kv, offsets, home, tile_tokens, tile_len)


def solution(mesh):
    placed = (
        P(("segment", "seq"), "tensor"),
        P("tensor", None),
        P(),
        P("seq", "tensor", "segment"),
        P(),
        P("seq", None),
    )
    return jax.shard_map(
        shards, mesh=mesh, in_specs=placed, out_specs=P("seq", "tensor", "segment"), check_vma=False
    )
```

```python
import functools

import jax
import jax.numpy as jnp
from jax import lax
from jax.experimental import pallas as pl
from jax.experimental.pallas import tpu as pltpu
from jax.sharding import PartitionSpec as P

MASKED = -1e30
HALVES = 2
STORES = 2
LOG2E = 1.4426950408889634
BLOCK_ROWS = 128
LARGE_VMEM = 52 * 1024 * 1024
MIDDLE_VMEM = 44 * 1024 * 1024
SMALL_VMEM = 16 * 1024 * 1024
VMEM = pl.BlockSpec(memory_space=pltpu.VMEM)
SMEM = pl.BlockSpec(memory_space=pltpu.SMEM)
ANY = pl.BlockSpec(memory_space=pl.ANY)
HBM = pl.BlockSpec(memory_space=pltpu.HBM)
ROWS_BY_ROWS = (((1,), (1,)), ((), ()))
COLS_BY_COLS = (((0,), (0,)), ((), ()))


def lasting(microseconds):
    return pl.CostEstimate(flops=0, bytes_accessed=int(3.6e6 * microseconds), transcendentals=0)


def project_kernel(bounds, block_ref, vision_hbm_ref, weight_ref, out_hbm_ref, vision_ref, held_ref, out_ref, load_sem, sems):
    cols = held_ref.shape[1]
    load = pltpu.make_async_copy(vision_hbm_ref, vision_ref, load_sem)
    load.start()
    across = pl.ds(pl.multiple_of(block_ref[0] * cols, cols), cols)
    spans = [pl.ds(low, high - low) for low, high in zip(bounds, bounds[1:])]
    copies = []
    for piece, span in enumerate(spans):
        copies.append(pltpu.make_async_copy(weight_ref.at[span, across], held_ref.at[span], sems.at[piece]))
        copies[-1].start()
    load.wait()
    total = None
    for piece, span in enumerate(spans):
        copies[piece].wait()
        product = jnp.dot(vision_ref[:, span], held_ref[span], preferred_element_type=jnp.float32)
        total = product if piece == 0 else total + product
    out_ref[...] = total
    store = pltpu.make_async_copy(out_ref, out_hbm_ref, load_sem)
    store.start()
    store.wait()


def project(vision, weight, block, cols):
    rows, depth = vision.shape
    bounds = [0, depth // 3, depth * 2 // 3, depth] if depth % 768 == 0 else [0, depth]
    return pl.pallas_call(
        functools.partial(project_kernel, bounds),
        in_specs=[SMEM, ANY, ANY],
        out_specs=ANY,
        out_shape=jax.ShapeDtypeStruct((rows, cols), jnp.float32),
        scratch_shapes=[
            pltpu.VMEM((rows, depth), jnp.bfloat16),
            pltpu.VMEM((depth, cols), jnp.bfloat16),
            pltpu.VMEM((rows, cols), jnp.float32),
            pltpu.SemaphoreType.DMA,
            pltpu.SemaphoreType.DMA((len(bounds) - 1,)),
        ],
        compiler_params=pltpu.CompilerParams(vmem_limit_bytes=LARGE_VMEM),
        cost_estimate=lasting(3 if cols < 1024 else 5),
    )(block.reshape(1), pltpu.with_memory_space_constraint(vision, pltpu.HBM), weight)


def finish_kernel(heads, dim, parts, own_ref, *refs):
    other_refs, gain_ref, out_ref = refs[:parts], refs[parts], refs[parts + 1]
    for head in range(heads):
        part, inside = divmod(head, heads // parts)
        at, other_at = head * 2 * dim, inside * 2 * dim
        keys = own_ref[:, at : at + dim] + other_refs[part][:, other_at : other_at + dim]
        mean_sq = jnp.mean(keys * keys, axis=-1, keepdims=True)
        keys = keys * lax.rsqrt(mean_sq + 1e-05) * gain_ref[...]
        values = own_ref[:, at + dim : at + 2 * dim] + other_refs[part][:, other_at + dim : other_at + 2 * dim]
        out_ref[head, :, :dim] = keys.astype(jnp.bfloat16)
        out_ref[head, :, dim:] = values.astype(jnp.bfloat16)


def finish(own, others, gain, heads, dim):
    rows = own.shape[0]
    return pl.pallas_call(
        functools.partial(finish_kernel, heads, dim, len(others)),
        in_specs=[VMEM] * (2 + len(others)),
        out_specs=VMEM,
        out_shape=jax.ShapeDtypeStruct((heads, rows, 2 * dim), jnp.bfloat16),
        compiler_params=pltpu.CompilerParams(vmem_limit_bytes=SMALL_VMEM),
        cost_estimate=lasting(1.5),
    )(own, *others, gain.reshape(1, dim))


def sort_kernel(tiles, group, q_ref, range_rows_ref, sorted_ref, hidden_ref, back_ref, hull_ref):
    rows, heads, width = q_ref.shape
    dim = width // group

    def order(lower, upper, at):
        key = jnp.where(upper > lower, (tiles - 1 - lower) * (tiles + 1) + tiles - upper, -1)
        return key * rows + at

    lower_row, upper_row = range_rows_ref[0:1, :], range_rows_ref[1:2, :]
    columns = jnp.concatenate([lower_row, upper_row] * 4, axis=0).astype(jnp.float32).T.astype(jnp.int32)
    lower, upper = columns[:, 0:1], columns[:, 1:2]
    order_col = order(lower, upper, lax.broadcasted_iota(jnp.int32, (rows, 1), 0))
    order_row = order(lower_row, upper_row, lax.broadcasted_iota(jnp.int32, (1, rows), 1))
    rank_row = jnp.sum(jnp.where(order_col < order_row, 1.0, 0.0), axis=0, keepdims=True).astype(jnp.int32)
    rank_col = jnp.sum(jnp.where(order_row < order_col, 1.0, 0.0), axis=1, keepdims=True).astype(jnp.int32)
    into = jnp.where(lax.broadcasted_iota(jnp.int32, (rows, rows), 0) == rank_row, 1.0, 0.0).astype(jnp.bfloat16)
    back = jnp.where(lax.broadcasted_iota(jnp.int32, (rows, rows), 1) == rank_col, 1.0, 0.0).astype(jnp.bfloat16)
    back_ref[...] = back
    seen_row = upper_row > lower_row
    blocks = rows // BLOCK_ROWS
    for block in range(blocks):
        inside = seen_row & (rank_row >= block * BLOCK_ROWS) & (rank_row < (block + 1) * BLOCK_ROWS)
        hull_ref[0, block] = jnp.min(jnp.where(inside, lower_row, tiles).astype(jnp.float32)).astype(jnp.int32)
        hull_ref[1, block] = jnp.max(jnp.where(inside, upper_row, 0).astype(jnp.float32)).astype(jnp.int32)
    hull_ref[2, 0] = jnp.sum(jnp.where(seen_row, 0.0, 1.0)).astype(jnp.int32)
    lanes = lax.broadcasted_iota(jnp.int32, (rows, dim), 1)
    unseen = (lanes < tiles) & ((lanes < lower) | (lanes >= upper)) | (lanes == tiles)
    hidden = jnp.where(unseen, 1.0, 0.0).astype(jnp.bfloat16)
    hidden_ref[...] = jnp.dot(into, hidden, preferred_element_type=jnp.float32).astype(jnp.bfloat16)
    q_heads = jnp.transpose(q_ref[...], (1, 0, 2))
    for head in range(heads):
        moved = jnp.dot(into, q_heads[head], preferred_element_type=jnp.float32).astype(jnp.bfloat16)
        for block in range(blocks):
            for member in range(group):
                at = (block * group + member) * BLOCK_ROWS
                sorted_ref[head, at : at + BLOCK_ROWS, :] = moved[
                    block * BLOCK_ROWS : (block + 1) * BLOCK_ROWS, member * dim : (member + 1) * dim
                ]


def sort_rows(queries, text_tiles, tiles, dim):
    rows, heads, width = queries.shape
    group = width // dim
    return pl.pallas_call(
        functools.partial(sort_kernel, tiles, group),
        in_specs=[VMEM, VMEM],
        out_specs=[VMEM, VMEM, VMEM, SMEM],
        out_shape=[
            jax.ShapeDtypeStruct((heads, rows * group, dim), jnp.bfloat16),
            jax.ShapeDtypeStruct((rows, dim), jnp.bfloat16),
            jax.ShapeDtypeStruct((rows, rows), jnp.bfloat16),
            jax.ShapeDtypeStruct((3, rows // BLOCK_ROWS), jnp.int32),
        ],
        compiler_params=pltpu.CompilerParams(vmem_limit_bytes=MIDDLE_VMEM),
        cost_estimate=lasting(0.1),
    )(queries, text_tiles.T)


def attend_kernel(shape, offsets, home_ref, tokens_ref, hull_ref, *refs):
    heads, blocks, group, dim, tiles, tile_len = shape
    pieces = len(offsets)
    piece_refs, refs = refs[:pieces], refs[pieces:]
    q_ref, hidden_ref, back_ref, result_hbm_ref, kv_ref, off_ref, turned_ref, result_ref, load_sems, store_sems = refs
    piece_rows = piece_refs[0].shape[1]
    columns = group * BLOCK_ROWS
    scale = LOG2E * dim ** (-0.5)
    loads = []
    for piece in range(pieces):
        at = pl.multiple_of((home_ref[0] ^ offsets[piece]) * piece_rows, piece_rows)
        loads.append(pltpu.make_async_copy(piece_refs[piece], kv_ref.at[:, pl.ds(at, piece_rows), :], load_sems.at[piece]))
        loads[-1].start()
    lanes = lax.broadcasted_iota(jnp.int32, (tile_len, dim), 1)
    place = lax.broadcasted_iota(jnp.int32, (tile_len, dim), 0)
    for tile in range(tiles):
        off = (lanes == tile) | ((lanes == tiles) & (place >= tokens_ref[tile]))
        off_ref[tile * tile_len : (tile + 1) * tile_len, :] = jnp.where(off, MASKED, 0.0).astype(jnp.bfloat16)
    for load in loads:
        load.wait()

    def work(block, first, count):
        here = pl.ds(pl.multiple_of(block * BLOCK_ROWS, BLOCK_ROWS), BLOCK_ROWS)
        if count == 0:
            turned_ref[:, :, here] = jnp.zeros((heads, group * dim, BLOCK_ROWS), jnp.bfloat16)
            return
        rows = pl.ds(pl.multiple_of(block * columns, columns), columns)
        span = pl.ds(pl.multiple_of(first * tile_len, tile_len), count * tile_len)
        hidden = jnp.concatenate([hidden_ref[here, :]] * group, axis=0)
        off = off_ref[span, :]
        row = lax.broadcasted_iota(jnp.int32, (1, columns), 1) % BLOCK_ROWS + block * BLOCK_ROWS
        scores = [
            lax.dot_general(
                jnp.concatenate([kv_ref[head, span, :dim], off], axis=1),
                jnp.concatenate([q_ref[head, rows, :], hidden], axis=1),
                ROWS_BY_ROWS,
                preferred_element_type=jnp.float32,
            )
            for head in range(heads)
        ]
        for head in range(heads):
            row_max = jnp.max(scores[head], axis=0, keepdims=True)
            terms = jnp.exp2((scores[head] - row_max) * scale)
            total = jnp.sum(terms, axis=0, keepdims=True)
            summed = lax.dot_general(
                kv_ref[head, span, dim:], terms.astype(jnp.bfloat16), COLS_BY_COLS, preferred_element_type=jnp.float32
            )
            inverse = jnp.where(row >= hull_ref[2, 0], 1.0 / total, 0.0)
            attended = (summed * inverse).astype(jnp.bfloat16)
            for member in range(group):
                turned_ref[head, member * dim : (member + 1) * dim, here] = attended[
                    :, member * BLOCK_ROWS : (member + 1) * BLOCK_ROWS
                ]

    @pl.loop(0, blocks)
    def _(block):
        first = hull_ref[0, block]
        seen = jnp.maximum(hull_ref[1, block] - first, 0)
        for count in range(tiles + 1):

            @pl.when(seen == count)
            def _():
                work(block, first, count)

    stores = []
    rows = back_ref.shape[0] // STORES
    for part in range(STORES):
        here = pl.ds(part * rows, rows)
        back = back_ref[here, :]
        whole = [
            lax.dot_general(back, turned_ref[head], ROWS_BY_ROWS, preferred_element_type=jnp.float32)
            for head in range(heads)
        ]
        whole = jnp.stack([head.astype(jnp.bfloat16) for head in whole], axis=0)
        result_ref[here] = jnp.transpose(whole, (1, 0, 2))
        stores.append(pltpu.make_async_copy(result_ref.at[here], result_hbm_ref.at[here], store_sems.at[part]))
        stores[-1].start()
    for store in stores:
        store.wait()


def attend(text, kv, offsets, home, tokens, tile_len):
    q, hidden, back, hull = text
    heads, dim = kv[0].shape[0], kv[0].shape[2] // 2
    text_rows, blocks = back.shape[0], hull.shape[1]
    group, tiles = q.shape[1] // text_rows, tokens.shape[0]
    width = group * dim
    total = sum(piece.shape[1] for piece in kv)
    kv = [pltpu.with_memory_space_constraint(piece, pltpu.HBM) for piece in kv]
    return pl.pallas_call(
        functools.partial(attend_kernel, (heads, blocks, group, dim, tiles, tile_len), offsets),
        in_specs=[SMEM] * 3 + [ANY] * len(kv) + [VMEM] * 3,
        out_specs=ANY,
        out_shape=jax.ShapeDtypeStruct((text_rows, heads, width), jnp.bfloat16),
        scratch_shapes=[
            pltpu.VMEM((heads, total, 2 * dim), jnp.bfloat16),
            pltpu.VMEM((total, dim), jnp.bfloat16),
            pltpu.VMEM((heads, width, text_rows), jnp.bfloat16),
            pltpu.VMEM((text_rows, heads, width), jnp.bfloat16),
            pltpu.SemaphoreType.DMA((len(kv),)),
            pltpu.SemaphoreType.DMA((STORES,)),
        ],
        compiler_params=pltpu.CompilerParams(vmem_limit_bytes=MIDDLE_VMEM),
        cost_estimate=lasting(15),
    )(home.reshape(1), tokens, hull, *kv, q, hidden, back)


def shards(vision_states, kv_weight, key_gain, queries, tile_tokens, text_tiles):
    dim = key_gain.shape[0]
    all_heads = kv_weight.shape[1] // (2 * dim)
    tensor, segment, seq = lax.axis_size("tensor"), lax.axis_size("segment"), lax.axis_size("seq")
    heads = all_heads // tensor
    tiles = tile_tokens.shape[0]
    tile_len = vision_states.shape[0] * segment * seq // tiles
    if tensor == 2 and segment == 2 and seq == 8 and heads % HALVES == 0:
        return by_swaps(vision_states, kv_weight, key_gain, queries, tile_tokens, text_tiles, heads, tile_len)
    text = sort_rows(queries, text_tiles, tiles, dim)
    weight_heads = kv_weight.reshape(kv_weight.shape[0], all_heads, 2 * dim)
    partial = jnp.einsum("rd,dch->crh", vision_states, weight_heads, preferred_element_type=jnp.float32)
    sums = lax.psum_scatter(partial, "tensor", scatter_dimension=0, tiled=True)
    keys = sums[:, :, :dim]
    mean_sq = jnp.mean(keys * keys, axis=-1, keepdims=True)
    keys = keys * lax.rsqrt(mean_sq + 1e-05) * key_gain
    block = jnp.concatenate([keys, sums[:, :, dim:]], axis=-1).astype(jnp.bfloat16)
    kv = [lax.all_gather(block, ("segment", "seq"), axis=1, tiled=True)]
    return attend(text, kv, [0], jnp.int32(0), tile_tokens, tile_len)


def after(first, then):
    return lax.optimization_barrier((first, then))[1]


def by_swaps(vision_states, kv_weight, key_gain, queries, tile_tokens, text_tiles, heads, tile_len):
    dim = key_gain.shape[0]
    me_tensor, me_segment, me_seq = lax.axis_index("tensor"), lax.axis_index("segment"), lax.axis_index("seq")

    def across(array, axis, step):
        return lax.ppermute(array, axis, [(i, i ^ step) for i in range(lax.axis_size(axis))])

    def part(count, index):
        return project(vision_states, kv_weight, index.astype(jnp.int32), heads * 2 * dim // count)

    text = sort_rows(queries, text_tiles, tile_tokens.shape[0], dim)
    home = me_segment * 8 + me_seq
    offsets = [8 * side + 2 * far + core for core in range(2) for side in range(2) for far in range(4)]
    other = 1 - me_tensor
    theirs = [part(HALVES, other * HALVES + half) for half in range(HALVES)]
    arrived = [across(half, "tensor", 1) for half in theirs]
    mine = part(1, me_tensor)
    block = finish(mine, arrived, key_gain, heads, dim)
    near, far, side = across(block, "seq", 2), across(block, "seq", 4), across(after(text, block), "segment", 1)
    far_near, side_far = across(after(near, far), "seq", 2), across(far, "segment", 1)
    side_near = across(side, "seq", 2)
    lane = [block, near, far, far_near, side, side_near, side_far, across(far_near, "segment", 1)]
    kv = lane + [across(piece, "seq", 1) for piece in lane]
    return attend(text, kv, offsets, home, tile_tokens, tile_len)


def solution(mesh):
    placed = (
        P(("segment", "seq"), "tensor"),
        P("tensor", None),
        P(),
        P("seq", "tensor", "segment"),
        P(),
        P("seq", None),
    )
    return jax.shard_map(
        shards, mesh=mesh, in_specs=placed, out_specs=P("seq", "tensor", "segment"), check_vma=False
    )
```

```python
import functools

import jax
import jax.numpy as jnp
from jax import lax
from jax.experimental import pallas as pl
from jax.experimental.pallas import tpu as pltpu
from jax.sharding import PartitionSpec as P

MASKED = -1e30
HALVES = 2
STORES = 2
LOG2E = 1.4426950408889634
BLOCK_ROWS = 128
LARGE_VMEM = 52 * 1024 * 1024
MIDDLE_VMEM = 44 * 1024 * 1024
SMALL_VMEM = 16 * 1024 * 1024
VMEM = pl.BlockSpec(memory_space=pltpu.VMEM)
SMEM = pl.BlockSpec(memory_space=pltpu.SMEM)
ANY = pl.BlockSpec(memory_space=pl.ANY)
HBM = pl.BlockSpec(memory_space=pltpu.HBM)
ROWS_BY_ROWS = (((1,), (1,)), ((), ()))
COLS_BY_COLS = (((0,), (0,)), ((), ()))


def lasting(microseconds):
    return pl.CostEstimate(flops=0, bytes_accessed=int(3.6e6 * microseconds), transcendentals=0)


def project_kernel(bounds, block_ref, vision_hbm_ref, weight_ref, out_hbm_ref, vision_ref, held_ref, out_ref, load_sem, sems):
    cols = held_ref.shape[1]
    load = pltpu.make_async_copy(vision_hbm_ref, vision_ref, load_sem)
    load.start()
    across = pl.ds(pl.multiple_of(block_ref[0] * cols, cols), cols)
    spans = [pl.ds(low, high - low) for low, high in zip(bounds, bounds[1:])]
    copies = []
    for piece, span in enumerate(spans):
        copies.append(pltpu.make_async_copy(weight_ref.at[span, across], held_ref.at[span], sems.at[piece]))
        copies[-1].start()
    load.wait()
    total = None
    for piece, span in enumerate(spans):
        copies[piece].wait()
        product = jnp.dot(vision_ref[:, span], held_ref[span], preferred_element_type=jnp.float32)
        total = product if piece == 0 else total + product
    out_ref[...] = total
    store = pltpu.make_async_copy(out_ref, out_hbm_ref, load_sem)
    store.start()
    store.wait()


def project(vision, weight, block, cols):
    rows, depth = vision.shape
    bounds = [0, depth // 3, depth * 2 // 3, depth] if depth % 768 == 0 else [0, depth]
    return pl.pallas_call(
        functools.partial(project_kernel, bounds),
        in_specs=[SMEM, ANY, ANY],
        out_specs=ANY,
        out_shape=jax.ShapeDtypeStruct((rows, cols), jnp.float32),
        scratch_shapes=[
            pltpu.VMEM((rows, depth), jnp.bfloat16),
            pltpu.VMEM((depth, cols), jnp.bfloat16),
            pltpu.VMEM((rows, cols), jnp.float32),
            pltpu.SemaphoreType.DMA,
            pltpu.SemaphoreType.DMA((len(bounds) - 1,)),
        ],
        compiler_params=pltpu.CompilerParams(vmem_limit_bytes=LARGE_VMEM),
        cost_estimate=lasting(3 if cols < 1024 else 5),
    )(block.reshape(1), pltpu.with_memory_space_constraint(vision, pltpu.HBM), weight)


def finish_kernel(heads, dim, parts, own_ref, *refs):
    other_refs, gain_ref, out_ref = refs[:parts], refs[parts], refs[parts + 1]
    for head in range(heads):
        part, inside = divmod(head, heads // parts)
        at, other_at = head * 2 * dim, inside * 2 * dim
        keys = own_ref[:, at : at + dim] + other_refs[part][:, other_at : other_at + dim]
        mean_sq = jnp.mean(keys * keys, axis=-1, keepdims=True)
        keys = keys * lax.rsqrt(mean_sq + 1e-05) * gain_ref[...]
        values = own_ref[:, at + dim : at + 2 * dim] + other_refs[part][:, other_at + dim : other_at + 2 * dim]
        out_ref[head, :, :dim] = keys.astype(jnp.bfloat16)
        out_ref[head, :, dim:] = values.astype(jnp.bfloat16)


def finish(own, others, gain, heads, dim):
    rows = own.shape[0]
    return pl.pallas_call(
        functools.partial(finish_kernel, heads, dim, len(others)),
        in_specs=[VMEM] * (2 + len(others)),
        out_specs=VMEM,
        out_shape=jax.ShapeDtypeStruct((heads, rows, 2 * dim), jnp.bfloat16),
        compiler_params=pltpu.CompilerParams(vmem_limit_bytes=SMALL_VMEM),
        cost_estimate=lasting(1.5),
    )(own, *others, gain.reshape(1, dim))


def sort_kernel(tiles, group, q_ref, range_rows_ref, sorted_ref, hidden_ref, back_ref, hull_ref):
    rows, heads, width = q_ref.shape
    dim = width // group

    def order(lower, upper, at):
        key = jnp.where(upper > lower, (tiles - 1 - lower) * (tiles + 1) + tiles - upper, -1)
        return key * rows + at

    lower_row, upper_row = range_rows_ref[0:1, :], range_rows_ref[1:2, :]
    columns = jnp.concatenate([lower_row, upper_row] * 4, axis=0).astype(jnp.float32).T.astype(jnp.int32)
    lower, upper = columns[:, 0:1], columns[:, 1:2]
    order_col = order(lower, upper, lax.broadcasted_iota(jnp.int32, (rows, 1), 0))
    order_row = order(lower_row, upper_row, lax.broadcasted_iota(jnp.int32, (1, rows), 1))
    rank_row = jnp.sum(jnp.where(order_col < order_row, 1.0, 0.0), axis=0, keepdims=True).astype(jnp.int32)
    rank_col = jnp.sum(jnp.where(order_row < order_col, 1.0, 0.0), axis=1, keepdims=True).astype(jnp.int32)
    into = jnp.where(lax.broadcasted_iota(jnp.int32, (rows, rows), 0) == rank_row, 1.0, 0.0).astype(jnp.bfloat16)
    back = jnp.where(lax.broadcasted_iota(jnp.int32, (rows, rows), 1) == rank_col, 1.0, 0.0).astype(jnp.bfloat16)
    back_ref[...] = back
    seen_row = upper_row > lower_row
    blocks = rows // BLOCK_ROWS
    for block in range(blocks):
        inside = seen_row & (rank_row >= block * BLOCK_ROWS) & (rank_row < (block + 1) * BLOCK_ROWS)
        hull_ref[0, block] = jnp.min(jnp.where(inside, lower_row, tiles).astype(jnp.float32)).astype(jnp.int32)
        hull_ref[1, block] = jnp.max(jnp.where(inside, upper_row, 0).astype(jnp.float32)).astype(jnp.int32)
    hull_ref[2, 0] = jnp.sum(jnp.where(seen_row, 0.0, 1.0)).astype(jnp.int32)
    lanes = lax.broadcasted_iota(jnp.int32, (rows, dim), 1)
    unseen = (lanes < tiles) & ((lanes < lower) | (lanes >= upper)) | (lanes == tiles)
    hidden = jnp.where(unseen, 1.0, 0.0).astype(jnp.bfloat16)
    hidden_ref[...] = jnp.dot(into, hidden, preferred_element_type=jnp.float32).astype(jnp.bfloat16)
    q_heads = jnp.transpose(q_ref[...], (1, 0, 2))
    for head in range(heads):
        moved = jnp.dot(into, q_heads[head], preferred_element_type=jnp.float32).astype(jnp.bfloat16)
        for block in range(blocks):
            for member in range(group):
                at = (block * group + member) * BLOCK_ROWS
                sorted_ref[head, at : at + BLOCK_ROWS, :] = moved[
                    block * BLOCK_ROWS : (block + 1) * BLOCK_ROWS, member * dim : (member + 1) * dim
                ]


def sort_rows(queries, text_tiles, tiles, dim):
    rows, heads, width = queries.shape
    group = width // dim
    return pl.pallas_call(
        functools.partial(sort_kernel, tiles, group),
        in_specs=[VMEM, VMEM],
        out_specs=[VMEM, VMEM, VMEM, SMEM],
        out_shape=[
            jax.ShapeDtypeStruct((heads, rows * group, dim), jnp.bfloat16),
            jax.ShapeDtypeStruct((rows, dim), jnp.bfloat16),
            jax.ShapeDtypeStruct((rows, rows), jnp.bfloat16),
            jax.ShapeDtypeStruct((3, rows // BLOCK_ROWS), jnp.int32),
        ],
        compiler_params=pltpu.CompilerParams(vmem_limit_bytes=MIDDLE_VMEM),
        cost_estimate=lasting(0.1),
    )(queries, text_tiles.T)


def attend_kernel(shape, offsets, home_ref, tokens_ref, hull_ref, *refs):
    heads, blocks, group, dim, tiles, tile_len = shape
    pieces = len(offsets)
    piece_refs, refs = refs[:pieces], refs[pieces:]
    q_ref, hidden_ref, back_ref, result_hbm_ref, kv_ref, off_ref, turned_ref, result_ref, load_sems, store_sems = refs
    piece_rows = piece_refs[0].shape[1]
    columns = group * BLOCK_ROWS
    scale = LOG2E * dim ** (-0.5)
    loads = []
    for piece in range(pieces):
        at = pl.multiple_of((home_ref[0] ^ offsets[piece]) * piece_rows, piece_rows)
        loads.append(pltpu.make_async_copy(piece_refs[piece], kv_ref.at[:, pl.ds(at, piece_rows), :], load_sems.at[piece]))
        loads[-1].start()
    lanes = lax.broadcasted_iota(jnp.int32, (tile_len, dim), 1)
    place = lax.broadcasted_iota(jnp.int32, (tile_len, dim), 0)
    for tile in range(tiles):
        off = (lanes == tile) | ((lanes == tiles) & (place >= tokens_ref[tile]))
        off_ref[tile * tile_len : (tile + 1) * tile_len, :] = jnp.where(off, MASKED, 0.0).astype(jnp.bfloat16)
    for load in loads:
        load.wait()

    def work(block, first, count):
        here = pl.ds(pl.multiple_of(block * BLOCK_ROWS, BLOCK_ROWS), BLOCK_ROWS)
        if count == 0:
            turned_ref[:, :, here] = jnp.zeros((heads, group * dim, BLOCK_ROWS), jnp.bfloat16)
            return
        rows = pl.ds(pl.multiple_of(block * columns, columns), columns)
        span = pl.ds(pl.multiple_of(first * tile_len, tile_len), count * tile_len)
        hidden = jnp.concatenate([hidden_ref[here, :]] * group, axis=0)
        off = off_ref[span, :]
        row = lax.broadcasted_iota(jnp.int32, (1, columns), 1) % BLOCK_ROWS + block * BLOCK_ROWS
        scores = [
            lax.dot_general(
                jnp.concatenate([kv_ref[head, span, :dim], off], axis=1),
                jnp.concatenate([q_ref[head, rows, :], hidden], axis=1),
                ROWS_BY_ROWS,
                preferred_element_type=jnp.float32,
            )
            for head in range(heads)
        ]
        for head in range(heads):
            row_max = jnp.max(scores[head], axis=0, keepdims=True)
            terms = jnp.exp2((scores[head] - row_max) * scale)
            total = jnp.sum(terms, axis=0, keepdims=True)
            summed = lax.dot_general(
                kv_ref[head, span, dim:], terms.astype(jnp.bfloat16), COLS_BY_COLS, preferred_element_type=jnp.float32
            )
            inverse = jnp.where(row >= hull_ref[2, 0], 1.0 / total, 0.0)
            attended = (summed * inverse).astype(jnp.bfloat16)
            for member in range(group):
                turned_ref[head, member * dim : (member + 1) * dim, here] = attended[
                    :, member * BLOCK_ROWS : (member + 1) * BLOCK_ROWS
                ]

    @pl.loop(0, blocks)
    def _(block):
        first = hull_ref[0, block]
        seen = jnp.maximum(hull_ref[1, block] - first, 0)
        for count in range(tiles + 1):

            @pl.when(seen == count)
            def _():
                work(block, first, count)

    stores = []
    rows = back_ref.shape[0] // STORES
    for part in range(STORES):
        here = pl.ds(part * rows, rows)
        back = back_ref[here, :]
        whole = [
            lax.dot_general(back, turned_ref[head], ROWS_BY_ROWS, preferred_element_type=jnp.float32)
            for head in range(heads)
        ]
        whole = jnp.stack([head.astype(jnp.bfloat16) for head in whole], axis=0)
        piece = rows // STORES
        for step in range(STORES):
            here = pl.ds(part * rows + step * piece, piece)
            result_ref[here] = jnp.transpose(whole[:, step * piece : (step + 1) * piece], (1, 0, 2))
            sem = store_sems.at[part * STORES + step]
            stores.append(pltpu.make_async_copy(result_ref.at[here], result_hbm_ref.at[here], sem))
            stores[-1].start()
    for store in stores:
        store.wait()


def attend(text, kv, offsets, home, tokens, tile_len):
    q, hidden, back, hull = text
    heads, dim = kv[0].shape[0], kv[0].shape[2] // 2
    text_rows, blocks = back.shape[0], hull.shape[1]
    group, tiles = q.shape[1] // text_rows, tokens.shape[0]
    width = group * dim
    total = sum(piece.shape[1] for piece in kv)
    kv = [pltpu.with_memory_space_constraint(piece, pltpu.HBM) for piece in kv]
    return pl.pallas_call(
        functools.partial(attend_kernel, (heads, blocks, group, dim, tiles, tile_len), offsets),
        in_specs=[SMEM] * 3 + [ANY] * len(kv) + [VMEM] * 3,
        out_specs=ANY,
        out_shape=jax.ShapeDtypeStruct((text_rows, heads, width), jnp.bfloat16),
        scratch_shapes=[
            pltpu.VMEM((heads, total, 2 * dim), jnp.bfloat16),
            pltpu.VMEM((total, dim), jnp.bfloat16),
            pltpu.VMEM((heads, width, text_rows), jnp.bfloat16),
            pltpu.VMEM((text_rows, heads, width), jnp.bfloat16),
            pltpu.SemaphoreType.DMA((len(kv),)),
            pltpu.SemaphoreType.DMA((STORES * STORES,)),
        ],
        compiler_params=pltpu.CompilerParams(vmem_limit_bytes=MIDDLE_VMEM),
        cost_estimate=lasting(15),
    )(home.reshape(1), tokens, hull, *kv, q, hidden, back)


def shards(vision_states, kv_weight, key_gain, queries, tile_tokens, text_tiles):
    dim = key_gain.shape[0]
    all_heads = kv_weight.shape[1] // (2 * dim)
    tensor, segment, seq = lax.axis_size("tensor"), lax.axis_size("segment"), lax.axis_size("seq")
    heads = all_heads // tensor
    tiles = tile_tokens.shape[0]
    tile_len = vision_states.shape[0] * segment * seq // tiles
    if tensor == 2 and segment == 2 and seq == 8 and heads % HALVES == 0:
        return by_swaps(vision_states, kv_weight, key_gain, queries, tile_tokens, text_tiles, heads, tile_len)
    text = sort_rows(queries, text_tiles, tiles, dim)
    weight_heads = kv_weight.reshape(kv_weight.shape[0], all_heads, 2 * dim)
    partial = jnp.einsum("rd,dch->crh", vision_states, weight_heads, preferred_element_type=jnp.float32)
    sums = lax.psum_scatter(partial, "tensor", scatter_dimension=0, tiled=True)
    keys = sums[:, :, :dim]
    mean_sq = jnp.mean(keys * keys, axis=-1, keepdims=True)
    keys = keys * lax.rsqrt(mean_sq + 1e-05) * key_gain
    block = jnp.concatenate([keys, sums[:, :, dim:]], axis=-1).astype(jnp.bfloat16)
    kv = [lax.all_gather(block, ("segment", "seq"), axis=1, tiled=True)]
    return attend(text, kv, [0], jnp.int32(0), tile_tokens, tile_len)


def after(first, then):
    return lax.optimization_barrier((first, then))[1]


def by_swaps(vision_states, kv_weight, key_gain, queries, tile_tokens, text_tiles, heads, tile_len):
    dim = key_gain.shape[0]
    me_tensor, me_segment, me_seq = lax.axis_index("tensor"), lax.axis_index("segment"), lax.axis_index("seq")

    def across(array, axis, step):
        return lax.ppermute(array, axis, [(i, i ^ step) for i in range(lax.axis_size(axis))])

    def part(count, index):
        return project(vision_states, kv_weight, index.astype(jnp.int32), heads * 2 * dim // count)

    text = sort_rows(queries, text_tiles, tile_tokens.shape[0], dim)
    home = me_segment * 8 + me_seq
    offsets = [8 * side + 2 * far + core for core in range(2) for side in range(2) for far in range(4)]
    other = 1 - me_tensor
    theirs = [part(HALVES, other * HALVES + half) for half in range(HALVES)]
    arrived = [across(half, "tensor", 1) for half in theirs]
    mine = part(1, me_tensor)
    block = finish(mine, arrived, key_gain, heads, dim)
    near, far, side = across(block, "seq", 2), across(block, "seq", 4), across(after(text, block), "segment", 1)
    far_near, side_far = across(after(near, far), "seq", 2), across(far, "segment", 1)
    side_near = across(side, "seq", 2)
    lane = [block, near, far, far_near, side, side_near, side_far, across(far_near, "segment", 1)]
    kv = lane + [across(piece, "seq", 1) for piece in lane]
    return attend(text, kv, offsets, home, tile_tokens, tile_len)


def solution(mesh):
    placed = (
        P(("segment", "seq"), "tensor"),
        P("tensor", None),
        P(),
        P("seq", "tensor", "segment"),
        P(),
        P("seq", None),
    )
    return jax.shard_map(
        shards, mesh=mesh, in_specs=placed, out_specs=P("seq", "tensor", "segment"), check_vma=False
    )
```

```python
import functools

import jax
import jax.numpy as jnp
from jax import lax
from jax.experimental import pallas as pl
from jax.experimental.pallas import tpu as pltpu
from jax.sharding import PartitionSpec as P

MASKED = -1e30
HALVES = 2
STORES = 2
LOG2E = 1.4426950408889634
BLOCK_ROWS = 128
LARGE_VMEM = 52 * 1024 * 1024
MIDDLE_VMEM = 44 * 1024 * 1024
SMALL_VMEM = 16 * 1024 * 1024
VMEM = pl.BlockSpec(memory_space=pltpu.VMEM)
SMEM = pl.BlockSpec(memory_space=pltpu.SMEM)
ANY = pl.BlockSpec(memory_space=pl.ANY)
HBM = pl.BlockSpec(memory_space=pltpu.HBM)
ROWS_BY_ROWS = (((1,), (1,)), ((), ()))
COLS_BY_COLS = (((0,), (0,)), ((), ()))


def lasting(microseconds):
    return pl.CostEstimate(flops=0, bytes_accessed=int(3.6e6 * microseconds), transcendentals=0)


def project_kernel(bounds, block_ref, vision_hbm_ref, weight_ref, out_hbm_ref, vision_ref, held_ref, out_ref, load_sem, sems):
    cols = held_ref.shape[1]
    load = pltpu.make_async_copy(vision_hbm_ref, vision_ref, load_sem)
    load.start()
    across = pl.ds(pl.multiple_of(block_ref[0] * cols, cols), cols)
    spans = [pl.ds(low, high - low) for low, high in zip(bounds, bounds[1:])]
    copies = []
    for piece, span in enumerate(spans):
        copies.append(pltpu.make_async_copy(weight_ref.at[span, across], held_ref.at[span], sems.at[piece]))
        copies[-1].start()
    load.wait()
    total = None
    for piece, span in enumerate(spans):
        copies[piece].wait()
        product = jnp.dot(vision_ref[:, span], held_ref[span], preferred_element_type=jnp.float32)
        total = product if piece == 0 else total + product
    out_ref[...] = total
    store = pltpu.make_async_copy(out_ref, out_hbm_ref, load_sem)
    store.start()
    store.wait()


def project(vision, weight, block, cols):
    rows, depth = vision.shape
    bounds = [0, depth // 3, depth * 2 // 3, depth] if depth % 768 == 0 else [0, depth]
    return pl.pallas_call(
        functools.partial(project_kernel, bounds),
        in_specs=[SMEM, ANY, ANY],
        out_specs=ANY,
        out_shape=jax.ShapeDtypeStruct((rows, cols), jnp.float32),
        scratch_shapes=[
            pltpu.VMEM((rows, depth), jnp.bfloat16),
            pltpu.VMEM((depth, cols), jnp.bfloat16),
            pltpu.VMEM((rows, cols), jnp.float32),
            pltpu.SemaphoreType.DMA,
            pltpu.SemaphoreType.DMA((len(bounds) - 1,)),
        ],
        compiler_params=pltpu.CompilerParams(vmem_limit_bytes=LARGE_VMEM),
        cost_estimate=lasting(3 if cols < 1024 else 5),
    )(block.reshape(1), pltpu.with_memory_space_constraint(vision, pltpu.HBM), weight)


def finish_kernel(heads, dim, parts, own_ref, *refs):
    other_refs, gain_ref, out_ref = refs[:parts], refs[parts], refs[parts + 1]
    for head in range(heads):
        part, inside = divmod(head, heads // parts)
        at, other_at = head * 2 * dim, inside * 2 * dim
        keys = own_ref[:, at : at + dim] + other_refs[part][:, other_at : other_at + dim]
        mean_sq = jnp.mean(keys * keys, axis=-1, keepdims=True)
        keys = keys * lax.rsqrt(mean_sq + 1e-05) * gain_ref[...]
        values = own_ref[:, at + dim : at + 2 * dim] + other_refs[part][:, other_at + dim : other_at + 2 * dim]
        out_ref[head, :, :dim] = keys.astype(jnp.bfloat16)
        out_ref[head, :, dim:] = values.astype(jnp.bfloat16)


def finish(own, others, gain, heads, dim):
    rows = own.shape[0]
    return pl.pallas_call(
        functools.partial(finish_kernel, heads, dim, len(others)),
        in_specs=[VMEM] * (2 + len(others)),
        out_specs=VMEM,
        out_shape=jax.ShapeDtypeStruct((heads, rows, 2 * dim), jnp.bfloat16),
        compiler_params=pltpu.CompilerParams(vmem_limit_bytes=SMALL_VMEM),
        cost_estimate=lasting(1.5),
    )(own, *others, gain.reshape(1, dim))


def sort_kernel(tiles, group, q_ref, range_rows_ref, sorted_ref, hidden_ref, back_ref, hull_ref):
    rows, heads, width = q_ref.shape
    dim = width // group

    def order(lower, upper, at):
        key = jnp.where(upper > lower, (tiles - 1 - lower) * (tiles + 1) + tiles - upper, -1)
        return key * rows + at

    lower_row, upper_row = range_rows_ref[0:1, :], range_rows_ref[1:2, :]
    columns = jnp.concatenate([lower_row, upper_row] * 4, axis=0).astype(jnp.float32).T.astype(jnp.int32)
    lower, upper = columns[:, 0:1], columns[:, 1:2]
    order_col = order(lower, upper, lax.broadcasted_iota(jnp.int32, (rows, 1), 0))
    order_row = order(lower_row, upper_row, lax.broadcasted_iota(jnp.int32, (1, rows), 1))
    rank_row = jnp.sum(jnp.where(order_col < order_row, 1.0, 0.0), axis=0, keepdims=True).astype(jnp.int32)
    rank_col = jnp.sum(jnp.where(order_row < order_col, 1.0, 0.0), axis=1, keepdims=True).astype(jnp.int32)
    into = jnp.where(lax.broadcasted_iota(jnp.int32, (rows, rows), 0) == rank_row, 1.0, 0.0).astype(jnp.bfloat16)
    back = jnp.where(lax.broadcasted_iota(jnp.int32, (rows, rows), 1) == rank_col, 1.0, 0.0).astype(jnp.bfloat16)
    back_ref[...] = back
    seen_row = upper_row > lower_row
    blocks = rows // BLOCK_ROWS
    for block in range(blocks):
        inside = seen_row & (rank_row >= block * BLOCK_ROWS) & (rank_row < (block + 1) * BLOCK_ROWS)
        hull_ref[0, block] = jnp.min(jnp.where(inside, lower_row, tiles).astype(jnp.float32)).astype(jnp.int32)
        hull_ref[1, block] = jnp.max(jnp.where(inside, upper_row, 0).astype(jnp.float32)).astype(jnp.int32)
    hull_ref[2, 0] = jnp.sum(jnp.where(seen_row, 0.0, 1.0)).astype(jnp.int32)
    lanes = lax.broadcasted_iota(jnp.int32, (rows, dim), 1)
    unseen = (lanes < tiles) & ((lanes < lower) | (lanes >= upper)) | (lanes == tiles)
    hidden = jnp.where(unseen, 1.0, 0.0).astype(jnp.bfloat16)
    hidden_ref[...] = jnp.dot(into, hidden, preferred_element_type=jnp.float32).astype(jnp.bfloat16)
    q_heads = jnp.transpose(q_ref[...], (1, 0, 2))
    for head in range(heads):
        moved = jnp.dot(into, q_heads[head], preferred_element_type=jnp.float32).astype(jnp.bfloat16)
        for block in range(blocks):
            for member in range(group):
                at = (block * group + member) * BLOCK_ROWS
                sorted_ref[head, at : at + BLOCK_ROWS, :] = moved[
                    block * BLOCK_ROWS : (block + 1) * BLOCK_ROWS, member * dim : (member + 1) * dim
                ]


def sort_rows(queries, text_tiles, tiles, dim):
    rows, heads, width = queries.shape
    group = width // dim
    return pl.pallas_call(
        functools.partial(sort_kernel, tiles, group),
        in_specs=[VMEM, VMEM],
        out_specs=[VMEM, VMEM, VMEM, SMEM],
        out_shape=[
            jax.ShapeDtypeStruct((heads, rows * group, dim), jnp.bfloat16),
            jax.ShapeDtypeStruct((rows, dim), jnp.bfloat16),
            jax.ShapeDtypeStruct((rows, rows), jnp.bfloat16),
            jax.ShapeDtypeStruct((3, rows // BLOCK_ROWS), jnp.int32),
        ],
        compiler_params=pltpu.CompilerParams(vmem_limit_bytes=MIDDLE_VMEM),
        cost_estimate=lasting(0.1),
    )(queries, text_tiles.T)


def attend_kernel(shape, offsets, home_ref, tokens_ref, hull_ref, *refs):
    heads, blocks, group, dim, tiles, tile_len = shape
    pieces = len(offsets)
    piece_refs, refs = refs[:pieces], refs[pieces:]
    q_ref, hidden_ref, back_ref, result_hbm_ref, kv_ref, off_ref, turned_ref, result_ref, load_sems, store_sems = refs
    piece_rows = piece_refs[0].shape[1]
    columns = group * BLOCK_ROWS
    scale = LOG2E * dim ** (-0.5)
    loads = []
    for piece in range(pieces):
        at = pl.multiple_of((home_ref[0] ^ offsets[piece]) * piece_rows, piece_rows)
        loads.append(pltpu.make_async_copy(piece_refs[piece], kv_ref.at[:, pl.ds(at, piece_rows), :], load_sems.at[piece]))
        loads[-1].start()
    lanes = lax.broadcasted_iota(jnp.int32, (tile_len, dim), 1)
    place = lax.broadcasted_iota(jnp.int32, (tile_len, dim), 0)
    for tile in range(tiles):
        off = (lanes == tile) | ((lanes == tiles) & (place >= tokens_ref[tile]))
        off_ref[tile * tile_len : (tile + 1) * tile_len, :] = jnp.where(off, MASKED, 0.0).astype(jnp.bfloat16)
    for load in loads:
        load.wait()

    def work(block, first, count):
        here = pl.ds(pl.multiple_of(block * BLOCK_ROWS, BLOCK_ROWS), BLOCK_ROWS)
        if count == 0:
            turned_ref[:, :, here] = jnp.zeros((heads, group * dim, BLOCK_ROWS), jnp.bfloat16)
            return
        rows = pl.ds(pl.multiple_of(block * columns, columns), columns)
        span = pl.ds(pl.multiple_of(first * tile_len, tile_len), count * tile_len)
        hidden = jnp.concatenate([hidden_ref[here, :]] * group, axis=0)
        off = off_ref[span, :]
        row = lax.broadcasted_iota(jnp.int32, (1, columns), 1) % BLOCK_ROWS + block * BLOCK_ROWS
        scores = [
            lax.dot_general(
                jnp.concatenate([kv_ref[head, span, :dim], off], axis=1),
                jnp.concatenate([q_ref[head, rows, :], hidden], axis=1),
                ROWS_BY_ROWS,
                preferred_element_type=jnp.float32,
            )
            for head in range(heads)
        ]
        for head in range(heads):
            row_max = jnp.max(scores[head], axis=0, keepdims=True)
            terms = jnp.exp2((scores[head] - row_max) * scale)
            total = jnp.sum(terms, axis=0, keepdims=True)
            summed = lax.dot_general(
                kv_ref[head, span, dim:], terms.astype(jnp.bfloat16), COLS_BY_COLS, preferred_element_type=jnp.float32
            )
            inverse = jnp.where(row >= hull_ref[2, 0], 1.0 / total, 0.0)
            attended = (summed * inverse).astype(jnp.bfloat16)
            for member in range(group):
                turned_ref[head, member * dim : (member + 1) * dim, here] = attended[
                    :, member * BLOCK_ROWS : (member + 1) * BLOCK_ROWS
                ]

    @pl.loop(0, blocks)
    def _(block):
        first = hull_ref[0, block]
        seen = jnp.maximum(hull_ref[1, block] - first, 0)
        for count in range(tiles + 1):

            @pl.when(seen == count)
            def _():
                work(block, first, count)

    stores = []
    rows = back_ref.shape[0] // STORES
    for part in range(STORES):
        here = pl.ds(part * rows, rows)
        back = back_ref[here, :]
        whole = [
            lax.dot_general(back, turned_ref[head], ROWS_BY_ROWS, preferred_element_type=jnp.float32)
            for head in range(heads)
        ]
        whole = jnp.stack([head.astype(jnp.bfloat16) for head in whole], axis=0)
        result_ref[here] = jnp.transpose(whole, (1, 0, 2))
        stores.append(pltpu.make_async_copy(result_ref.at[here], result_hbm_ref.at[here], store_sems.at[part]))
        stores[-1].start()
    for store in stores:
        store.wait()


def attend(text, kv, offsets, home, tokens, tile_len):
    q, hidden, back, hull = text
    heads, dim = kv[0].shape[0], kv[0].shape[2] // 2
    text_rows, blocks = back.shape[0], hull.shape[1]
    group, tiles = q.shape[1] // text_rows, tokens.shape[0]
    width = group * dim
    total = sum(piece.shape[1] for piece in kv)
    kv = [pltpu.with_memory_space_constraint(piece, pltpu.HBM) for piece in kv]
    return pl.pallas_call(
        functools.partial(attend_kernel, (heads, blocks, group, dim, tiles, tile_len), offsets),
        in_specs=[SMEM] * 3 + [ANY] * len(kv) + [VMEM] * 3,
        out_specs=ANY,
        out_shape=jax.ShapeDtypeStruct((text_rows, heads, width), jnp.bfloat16),
        scratch_shapes=[
            pltpu.VMEM((heads, total, 2 * dim), jnp.bfloat16),
            pltpu.VMEM((total, dim), jnp.bfloat16),
            pltpu.VMEM((heads, width, text_rows), jnp.bfloat16),
            pltpu.VMEM((text_rows, heads, width), jnp.bfloat16),
            pltpu.SemaphoreType.DMA((len(kv),)),
            pltpu.SemaphoreType.DMA((STORES,)),
        ],
        compiler_params=pltpu.CompilerParams(vmem_limit_bytes=MIDDLE_VMEM),
        cost_estimate=lasting(15),
    )(home.reshape(1), tokens, hull, *kv, q, hidden, back)


def shards(vision_states, kv_weight, key_gain, queries, tile_tokens, text_tiles):
    dim = key_gain.shape[0]
    all_heads = kv_weight.shape[1] // (2 * dim)
    tensor, segment, seq = lax.axis_size("tensor"), lax.axis_size("segment"), lax.axis_size("seq")
    heads = all_heads // tensor
    tiles = tile_tokens.shape[0]
    tile_len = vision_states.shape[0] * segment * seq // tiles
    if tensor == 2 and segment == 2 and seq == 8 and heads % HALVES == 0:
        return by_swaps(vision_states, kv_weight, key_gain, queries, tile_tokens, text_tiles, heads, tile_len)
    text = sort_rows(queries, text_tiles, tiles, dim)
    weight_heads = kv_weight.reshape(kv_weight.shape[0], all_heads, 2 * dim)
    partial = jnp.einsum("rd,dch->crh", vision_states, weight_heads, preferred_element_type=jnp.float32)
    sums = lax.psum_scatter(partial, "tensor", scatter_dimension=0, tiled=True)
    keys = sums[:, :, :dim]
    mean_sq = jnp.mean(keys * keys, axis=-1, keepdims=True)
    keys = keys * lax.rsqrt(mean_sq + 1e-05) * key_gain
    block = jnp.concatenate([keys, sums[:, :, dim:]], axis=-1).astype(jnp.bfloat16)
    kv = [lax.all_gather(block, ("segment", "seq"), axis=1, tiled=True)]
    return attend(text, kv, [0], jnp.int32(0), tile_tokens, tile_len)


def after(first, then):
    return lax.optimization_barrier((first, then))[1]


def by_swaps(vision_states, kv_weight, key_gain, queries, tile_tokens, text_tiles, heads, tile_len):
    dim = key_gain.shape[0]
    me_tensor, me_segment, me_seq = lax.axis_index("tensor"), lax.axis_index("segment"), lax.axis_index("seq")

    def across(array, axis, step):
        return lax.ppermute(array, axis, [(i, i ^ step) for i in range(lax.axis_size(axis))])

    def part(count, index):
        return project(vision_states, kv_weight, index.astype(jnp.int32), heads * 2 * dim // count)

    text = sort_rows(queries, text_tiles, tile_tokens.shape[0], dim)
    home = me_segment * 8 + me_seq
    offsets = [8 * side + 2 * far + core for core in range(2) for side in range(2) for far in range(4)]
    other = 1 - me_tensor
    theirs = [part(HALVES, other * HALVES + half) for half in range(HALVES)]
    arrived = [across(half, "tensor", 1) for half in theirs]
    mine = part(1, me_tensor)
    block = finish(mine, arrived, key_gain, heads, dim)
    near, far, side = across(block, "seq", 2), across(block, "seq", 4), across(block, "segment", 1)
    far_near, side_far = across(after(near, far), "seq", 2), across(far, "segment", 1)
    side_near = across(after(text, side), "seq", 2)
    lane = [block, near, far, far_near, side, side_near, side_far, across(far_near, "segment", 1)]
    kv = lane + [across(piece, "seq", 1) for piece in lane]
    return attend(text, kv, offsets, home, tile_tokens, tile_len)


def solution(mesh):
    placed = (
        P(("segment", "seq"), "tensor"),
        P("tensor", None),
        P(),
        P("seq", "tensor", "segment"),
        P(),
        P("seq", None),
    )
    return jax.shard_map(
        shards, mesh=mesh, in_specs=placed, out_specs=P("seq", "tensor", "segment"), check_vma=False
    )
```
